128 devices in a mesh: node: 16 (over y, z), chip: 8 (over x, core).
Axes of the slice: x: 4, y: 4, z: 4, core: 2. Of those that a mesh axis runs over, the one named last changes fastest.
Arguments:
- tokens: bfloat16 [32768, 2048], P(('node', 'chip')), may hold values from -6 to 6
- cotangent: bfloat16 [32768, 2048], P(('node', 'chip')), may hold values from -6 to 6
- chosen_rows: int32 [128, 256], P(('node', 'chip')), may hold values from 0 to 32767, as said below
- sensor_group: int32 [128], P(('node', 'chip')), may hold values from 0 to 3, as said below
- router: bfloat16 [128, 2048], P(('node', 'chip')), may hold values from -0.125 to 0.125
- gate_weight: bfloat16 [128, 2048, 1408], P(('node', 'chip')), may hold values from -0.125 to 0.125
- up_weight: bfloat16 [128, 2048, 1408], P(('node', 'chip')), may hold values from -0.125 to 0.125
- down_weight: bfloat16 [128, 1408, 2048], P(('node', 'chip')), may hold values from -0.15625 to 0.15625
Outputs:
- token_grad: bfloat16 [32768, 2048], P(('node', 'chip'))
- down_grad: bfloat16 [128, 1408, 2048], P(('node', 'chip'))
- router_grad: float32 [128, 2048], P(('node', 'chip'))
The draws below stay inside these ranges and needn't reach their ends.
Inputs may be any that keep to these rules, and one draw needn't show every extreme that they name: `chosen_rows`: only the first 256 // 2**sensor_group[e] slots of expert e are live. The live picks of one expert are distinct rows, and at most 2 of them lie among the rows of one device (rows d * 256 to (d + 1) * 256 - 1); in every draw some expert takes exactly 2 rows from every device. For every device and every c, at most 8 of the experts e with e % 8 == c have live picks among that device's rows, and in every draw some device reaches 8. `sensor_group`: every sensor type names exactly 32 experts.
All inputs are finite; a program needn't handle non-finite values.
Results may differ from the reference program's by a relative error of at most 0.006.
Values may be sent and summed in bfloat16 or wider, within the bound.
A program may use at most 128 MiB of HBM per device.

```python
import jax
import jax.numpy as jnp
from jax import lax

D = 2048
FF = 1408
GROUPS = 4
MOST = 2
ROWS_DEV = 256
EXPERTS = 128
CAP = 256
TOKENS = 32768
N_NODE = 16
N_CHIP = 8


def layout_order(key):
    order_key = jax.random.fold_in(key, 5)
    return jax.vmap(lambda subkey: jax.random.permutation(subkey, N_NODE))(jax.random.split(order_key, N_CHIP)).astype(jnp.int32)


def draw_chosen_rows(key, part):
    order = layout_order(key)
    key = jax.random.fold_in(key, 11)
    table_key, score_key = jax.random.split(key)
    flat_order = order.T.reshape(-1)
    group_of = flat_order % GROUPS
    place_in = flat_order // GROUPS
    column_of = jnp.arange(EXPERTS, dtype=jnp.int32) % N_CHIP
    tables = jax.vmap(lambda subkey: jax.random.permutation(subkey, EXPERTS))(jax.random.split(table_key, N_CHIP * GROUPS))
    tables = tables.astype(jnp.int32).reshape(N_CHIP, GROUPS, EXPERTS)
    span = jnp.right_shift(jnp.full((EXPERTS,), EXPERTS, jnp.int32), group_of)
    position = (place_in[:, None] * span[:, None] + jnp.arange(EXPERTS, dtype=jnp.int32)[None, :]) % EXPERTS
    sources = tables[column_of[:, None], group_of[:, None], position]
    scores = jax.random.randint(score_key, (EXPERTS, EXPERTS, ROWS_DEV), 0, 2 ** 20) * ROWS_DEV
    scores = scores + jnp.arange(ROWS_DEV, dtype=jnp.int32)[None, None, :]
    within = lax.top_k(scores, MOST)[1].astype(jnp.int32)
    slot_index = jnp.arange(CAP, dtype=jnp.int32)
    source_dev = sources[:, slot_index // MOST].astype(jnp.int32)
    rank_index = slot_index % MOST
    expert_index = jnp.arange(EXPERTS, dtype=jnp.int32)[:, None]
    local_row = within[expert_index, source_dev, rank_index[None, :]]
    return (source_dev * ROWS_DEV + local_row).astype(jnp.int32)


def draw_sensor_group(key, part):
    order = layout_order(key)
    return (order.T.reshape(-1) % GROUPS).astype(jnp.int32)


def levels(own_key, dims, pieces, smallest, high):
    level, own = 1.0, jax.random.fold_in(own_key, 6)
    for dim, blocks in pieces:
        heights = jnp.exp(jax.random.uniform(jax.random.fold_in(own, dim), (blocks,), jnp.float32, smallest / len(pieces), high / len(pieces)))
        level = level * jnp.repeat(heights, dims[dim] // blocks).reshape([-1 if axis == dim else 1 for axis in range(len(dims))])
    return level


def scatter_about(stream_key, shape, width, most, cuts=(), kind=jnp.bfloat16):
    factor_of = levels(stream_key, shape, cuts, -0.22, 0.18) if cuts else 1.0
    values = jax.random.normal(stream_key, shape, jnp.float32) * width * factor_of
    return jnp.minimum(jnp.maximum(values, -most), most).astype(kind)


def setup_inputs(seed: int = 0) -> dict:
    arg_keys = jax.random.split(jax.random.key(seed), 9)
    tokens = scatter_about(arg_keys[0], (TOKENS, D), 1.0, 6.0, ((0, 128),))
    cotangent = scatter_about(arg_keys[1], (TOKENS, D), 1.0, 6.0, ((0, 128),))
    chosen_rows = draw_chosen_rows(jax.random.fold_in(arg_keys[8], 71), 0)
    sensor_group = draw_sensor_group(jax.random.fold_in(arg_keys[8], 71), 0)
    router = scatter_about(arg_keys[4], (EXPERTS, D), D ** -0.5, 0.125, ((0, 128),))
    gate_weight = scatter_about(arg_keys[5], (EXPERTS, D, FF), D ** -0.5, 0.125, ((0, 128),))
    up_weight = scatter_about(arg_keys[6], (EXPERTS, D, FF), D ** -0.5, 0.125, ((0, 128),))
    down_weight = scatter_about(arg_keys[7], (EXPERTS, FF, D), FF ** -0.5, 0.15625, ((0, 128),))
    return dict(tokens=tokens, cotangent=cotangent, chosen_rows=chosen_rows, sensor_group=sensor_group, router=router, gate_weight=gate_weight, up_weight=up_weight, down_weight=down_weight)


def expert_backward(x_rows, dy_rows, router_row, w_gate, w_up, w_down):
    pre_gate = jnp.dot(x_rows, w_gate, preferred_element_type=jnp.float32)
    pre_up = jnp.dot(x_rows, w_up, preferred_element_type=jnp.float32)
    gate_sig = jax.nn.sigmoid(pre_gate)
    gate_act = pre_gate * gate_sig
    hidden = (gate_act * pre_up).astype(jnp.bfloat16)
    expert_out = jnp.dot(hidden, w_down, preferred_element_type=jnp.float32)
    score = jax.nn.sigmoid(jnp.dot(x_rows, router_row, preferred_element_type=jnp.float32))
    weight_grad = jnp.sum(dy_rows.astype(jnp.float32) * expert_out, axis=1)
    score_grad = weight_grad * score * (1.0 - score)
    out_grad = (score[:, None] * dy_rows.astype(jnp.float32)).astype(jnp.bfloat16)
    down_grad = jnp.dot(hidden.T, out_grad, preferred_element_type=jnp.float32).astype(jnp.bfloat16)
    hidden_grad = jnp.dot(out_grad, w_down.T, preferred_element_type=jnp.float32)
    gate_grad = (hidden_grad * pre_up * gate_sig * (1.0 + pre_gate * (1.0 - gate_sig))).astype(jnp.bfloat16)
    up_grad = (hidden_grad * gate_act).astype(jnp.bfloat16)
    pick_grad = jnp.dot(gate_grad, w_gate.T, preferred_element_type=jnp.float32)
    pick_grad = pick_grad + jnp.dot(up_grad, w_up.T, preferred_element_type=jnp.float32)
    pick_grad = pick_grad + score_grad[:, None] * router_row.astype(jnp.float32)[None, :]
    router_grad = jnp.dot(score_grad, x_rows.astype(jnp.float32), precision=lax.Precision.HIGHEST)
    return pick_grad.astype(jnp.bfloat16), down_grad, router_grad


def reference(tokens, cotangent, chosen_rows, sensor_group, router, gate_weight, up_weight, down_weight):
    live_count = jnp.right_shift(jnp.full((EXPERTS,), CAP, jnp.int32), sensor_group.astype(jnp.int32))
    live = jnp.arange(CAP, dtype=jnp.int32)[None, :] < live_count[:, None]

    def per_expert(inputs):
        row_ids, alive, router_row, w_gate, w_up, w_down = inputs
        x_rows = jnp.where(alive[:, None], tokens[row_ids], jnp.zeros((), tokens.dtype))
        dy_rows = jnp.where(alive[:, None], cotangent[row_ids], jnp.zeros((), cotangent.dtype))
        return expert_backward(x_rows, dy_rows, router_row, w_gate, w_up, w_down)

    pick_grads, down_grads, router_grads = lax.map(per_expert, (chosen_rows, live, router, gate_weight, up_weight, down_weight))
    summed = jnp.zeros((TOKENS, D), jnp.float32).at[chosen_rows.reshape(-1)].add(pick_grads.reshape(-1, D).astype(jnp.float32))
    return summed.astype(jnp.bfloat16), down_grads, router_grads
```

```python
import functools

import jax
import jax.numpy as jnp
from jax import lax
from jax.experimental import pallas as pl
from jax.experimental.pallas import tpu as pltpu
from jax.sharding import PartitionSpec as P

MESH = pl.DeviceIdType.MESH
F32 = jnp.float32
BF16 = jnp.bfloat16
BLOCK = 16
STEPS = 4


def dot(a, b):
    return jnp.dot(a, b, preferred_element_type=F32)


def dot_nt(a, b):
    return lax.dot_general(a, b, (((1,), (1,)), ((), ())), preferred_element_type=F32)


def exchange_kernel(
    n_node,
    n_chip,
    chosen,
    group,
    router,
    tokens,
    cotangent,
    w_gate_hbm,
    w_up_hbm,
    w_down_hbm,
    ret_out,
    scatter_out,
    hidden_t_out,
    out_grad_out,
    router_grad,
    both,
    w_gate,
    w_up,
    w_down,
    list_send,
    lists,
    expand,
    compact,
    pick_send,
    pick_mine,
    stage_a,
    mid,
    stage_b,
    rows,
    pre_gate,
    pre_up,
    raw,
    score,
    hidden,
    hidden_t,
    gate_grad,
    up_grad,
    score_grad,
    out_grad,
    back,
    back_mid,
    back_stage,
    ret,
    scatter,
    load_sem,
    store_sem,
    list_sem,
    pick_sem,
    a_send,
    a_recv,
    b_send,
    b_recv,
    rb_send,
    rb_recv,
    ra_send,
    ra_recv,
):
    n = lax.axis_index("node")
    c = lax.axis_index("chip")
    width = router.shape[1]
    ff = w_gate.shape[1]
    chunk = width // STEPS
    dense = n_node * BLOCK
    packed = n_chip * BLOCK

    loads = [
        pltpu.make_async_copy(tokens, both.at[:, pl.ds(0, width)], load_sem.at[0]),
        pltpu.make_async_copy(cotangent, both.at[:, pl.ds(width, width)], load_sem.at[1]),
        pltpu.make_async_copy(w_gate_hbm, w_gate, load_sem.at[2]),
        pltpu.make_async_copy(w_up_hbm, w_up, load_sem.at[3]),
        pltpu.make_async_copy(w_down_hbm, w_down, load_sem.at[4]),
    ]
    for load in loads:
        load.start()

    def node_peer(i):
        return lax.rem(n + i, n_node)

    def chip_peer(i):
        return lax.rem(c + i, n_chip)

    barrier = pltpu.get_barrier_semaphore()

    def greet_node(i, carry):
        pl.semaphore_signal(barrier, inc=1, device_id=(node_peer(i), c), device_id_type=MESH)
        return carry

    def greet_chip(i, carry):
        pl.semaphore_signal(barrier, inc=1, device_id=(n, chip_peer(i)), device_id_type=MESH)
        return carry

    lax.fori_loop(1, n_node, greet_node, 0)
    lax.fori_loop(1, n_chip, greet_chip, 0)

    cap = chosen.shape[1]
    slot_index = lax.broadcasted_iota(jnp.int32, (8, cap), 1)
    live = jnp.right_shift(jnp.full((8, cap), cap, jnp.int32), jnp.broadcast_to(group[...], (8, cap)))
    own_list = jnp.where(slot_index < live, jnp.broadcast_to(chosen[...], (8, cap)), -1)
    list_send[...] = own_list
    lists[pl.ds(pl.multiple_of(n * 8, 8), 8), :] = own_list

    pl.semaphore_wait(barrier, n_node + n_chip - 2)

    def send_list(i, carry):
        pltpu.make_async_remote_copy(
            src_ref=list_send,
            dst_ref=lists.at[pl.ds(pl.multiple_of(n * 8, 8), 8), :],
            send_sem=list_sem.at[0],
            recv_sem=list_sem.at[1],
            device_id=(node_peer(i), c),
            device_id_type=MESH,
        ).start()
        return carry

    lax.fori_loop(1, n_node, send_list, 0)

    pre_gate[...] = jnp.zeros_like(pre_gate)
    pre_up[...] = jnp.zeros_like(pre_up)
    raw[...] = jnp.zeros_like(raw)
    score[...] = jnp.zeros_like(score)

    def wait_bytes(ref, sem):
        pltpu.make_async_copy(ref, ref, sem).wait()

    wait_bytes(lists.at[pl.ds(0, (n_node - 1) * 8), :], list_sem.at[0])
    wait_bytes(lists.at[pl.ds(0, (n_node - 1) * 8), :], list_sem.at[1])

    source = lax.broadcasted_iota(jnp.int32, (8, 1), 0)
    lane_row = lax.broadcasted_iota(jnp.int32, (8, cap), 1)
    lane_slot = lax.broadcasted_iota(jnp.int32, (8, packed), 1)
    used = jnp.zeros((8, 1), jnp.int32)
    expand_parts, row_parts = [], []
    for e in range(n_node):
        listed = lists[8 * e : 8 * e + 8, :]
        mine = jnp.right_shift(listed, 8) == n * n_chip + source
        local_row = jnp.bitwise_and(listed, 255)
        low = jnp.min(jnp.where(mine, local_row, 256), axis=1, keepdims=True)
        high = jnp.max(jnp.where(mine, local_row, -1), axis=1, keepdims=True)
        place = source * BLOCK + used
        first = jnp.where(high >= 0, place, -1)
        second = jnp.where(high > low, place + 8, -1)
        expand_parts.append(jnp.where(lane_slot == first, 1.0, 0.0))
        expand_parts.append(jnp.where(lane_slot == second, 1.0, 0.0))
        row_parts.append(jnp.where(lane_row == low, 1.0, 0.0))
        row_parts.append(jnp.where(lane_row == high, 1.0, 0.0))
        used = used + jnp.where(high >= 0, 1, 0)
    expand_f32 = jnp.concatenate(expand_parts, axis=0)
    expand[...] = expand_f32.astype(BF16)
    compact[...] = expand_f32.T.astype(BF16)
    row_hot = jnp.concatenate(row_parts, axis=0).astype(BF16)
    pick_send[...] = dot(compact[...], row_hot).astype(BF16)

    def block(i):
        return pl.ds(pl.multiple_of(i * BLOCK, BLOCK), BLOCK)

    def send_pick(i, carry):
        to = chip_peer(i)
        pltpu.make_async_remote_copy(
            src_ref=pick_send.at[block(to), :],
            dst_ref=pick_mine.at[block(c), :],
            send_sem=pick_sem.at[0],
            recv_sem=pick_sem.at[1],
            device_id=(n, to),
            device_id_type=MESH,
        ).start()
        return carry

    lax.fori_loop(1, n_chip, send_pick, 0)
    pick_mine[block(c), :] = pick_send[block(c), :]
    loads[0].wait()
    loads[1].wait()
    wait_bytes(pick_mine.at[pl.ds(0, (n_chip - 1) * BLOCK), :], pick_sem.at[0])
    wait_bytes(pick_mine.at[pl.ds(0, (n_chip - 1) * BLOCK), :], pick_sem.at[1])

    def cols(s):
        return pl.ds(pl.multiple_of(s * chunk, chunk), chunk)

    def to_chips(src, dst, s, send_sem, recv_sem):
        def one(i, carry):
            to = chip_peer(i)
            pltpu.make_async_remote_copy(
                src_ref=src.at[block(to), cols(s)],
                dst_ref=dst.at[block(c), cols(s)],
                send_sem=send_sem.at[s],
                recv_sem=recv_sem.at[s],
                device_id=(n, to),
                device_id_type=MESH,
            ).start()
            return carry

        lax.fori_loop(1, n_chip, one, 0)
        dst[block(c), cols(s)] = src[block(c), cols(s)]

    def to_nodes(src, dst, s, send_sem, recv_sem):
        def one(i, carry):
            to = node_peer(i)
            pltpu.make_async_remote_copy(
                src_ref=src.at[block(to), cols(s)],
                dst_ref=dst.at[block(n), cols(s)],
                send_sem=send_sem.at[s],
                recv_sem=recv_sem.at[s],
                device_id=(to, c),
                device_id_type=MESH,
            ).start()
            return carry

        lax.fori_loop(1, n_node, one, 0)
        dst[block(n), cols(s)] = src[block(n), cols(s)]

    def chips_done(ref, s, sem):
        wait_bytes(ref.at[pl.ds(0, packed - BLOCK), cols(s)], sem.at[s])

    def nodes_done(ref, s, sem):
        wait_bytes(ref.at[pl.ds(0, dense - BLOCK), cols(s)], sem.at[s])

    def gather(s):
        stage_a[:, cols(s)] = dot(pick_mine[...], both[:, cols(s)]).astype(BF16)
        to_chips(stage_a, mid, s, a_send, a_recv)

    def forward(s):
        chips_done(mid, s, a_recv)
        stage_b[:, cols(s)] = dot(expand[...], mid[:, cols(s)]).astype(BF16)
        to_nodes(stage_b, rows, s, b_send, b_recv)

    def up_step(s):
        nodes_done(rows, s, b_recv)
        x = rows[:, cols(s)]
        pre_gate[...] += dot(x, w_gate[cols(s), :])
        pre_up[...] += dot(x, w_up[cols(s), :])
        score[...] += dot_nt(x, jnp.broadcast_to(router[:, cols(s)], (128, chunk)))

    def down_step(s):
        nodes_done(rows, s, b_recv)
        raw[...] += dot_nt(rows[:, cols(s)], w_down[:, cols(s - STEPS)])

    gather(0)
    scatter[...] = pick_mine[...].astype(F32).T.astype(BF16)
    scatter_store = pltpu.make_async_copy(scatter, scatter_out, store_sem.at[0])
    scatter_store.start()
    gather(1)
    forward(0)
    loads[2].wait()
    loads[3].wait()

    def x_phase(s, carry):
        gather(s + 1)
        forward(s)
        up_step(s - 1)
        return carry

    lax.fori_loop(1, STEPS + 1, x_phase, 0)

    def from_x(r, carry):
        part = pl.ds(pl.multiple_of(r * 64, 64), 64)
        s = jax.nn.sigmoid(score[part, :])
        score[part, :] = s
        for j in range(ff // 128):
            lanes = pl.ds(128 * j, 128)
            g = pre_gate[part, lanes]
            u = pre_up[part, lanes]
            sig = jax.nn.sigmoid(g)
            act = g * sig
            hidden[part, lanes] = (act * u).astype(BF16)
            pre_gate[part, lanes] = s * (u * sig * (1.0 + g * (1.0 - sig)))
            pre_up[part, lanes] = s * act
        return carry

    lax.fori_loop(0, dense // 64, from_x, 0)
    loads[4].wait()

    def dy_phase(s, carry):
        @pl.when(s + 1 < 2 * STEPS)
        def _():
            gather(s + 1)

        forward(s)
        down_step(s - 1)
        return carry

    lax.fori_loop(STEPS + 1, 2 * STEPS, dy_phase, 0)
    down_step(2 * STEPS - 1)

    def from_dy(r, carry):
        part = pl.ds(pl.multiple_of(r * 64, 64), 64)
        total = jnp.zeros((64, 128), F32)
        for j in range(ff // 128):
            lanes = pl.ds(128 * j, 128)
            v = raw[part, lanes]
            total = total + v * hidden[part, lanes].astype(F32)
            gate_grad[part, lanes] = (v * pre_gate[part, lanes]).astype(BF16)
            up_grad[part, lanes] = (v * pre_up[part, lanes]).astype(BF16)
        s = score[part, :]
        score_grad[part, :] = jnp.sum(total, axis=1, keepdims=True) * s * (1.0 - s)
        return carry

    lax.fori_loop(0, dense // 64, from_dy, 0)

    def send_back(s):
        value = dot_nt(gate_grad[...], w_gate[cols(s), :])
        value = value + dot_nt(up_grad[...], w_up[cols(s), :])
        value = value + score_grad[:, :1] * router[:, cols(s)].astype(F32)
        back[:, cols(s)] = value.astype(BF16)
        to_nodes(back, back_mid, s, rb_send, rb_recv)

    def send_home(s):
        nodes_done(back_mid, s, rb_recv)
        back_stage[:, cols(s)] = dot(compact[...], back_mid[:, cols(s)]).astype(BF16)
        to_chips(back_stage, ret, s, ra_send, ra_recv)

    send_back(0)
    hidden_t[...] = hidden[...].astype(F32).T.astype(BF16)
    hidden_store = pltpu.make_async_copy(hidden_t, hidden_t_out, store_sem.at[1])
    hidden_store.start()

    def return_phase(s, carry):
        send_back(s)
        send_home(s - 1)
        return carry

    lax.fori_loop(1, STEPS, return_phase, 0)

    def scale(r, carry):
        part = pl.ds(pl.multiple_of(r * 16, 16), 16)
        s = score[part, :1]
        out_grad[part, :] = (s * rows[part, width:].astype(F32)).astype(BF16)
        return carry

    lax.fori_loop(0, dense // 16, scale, 0)
    grad_store = pltpu.make_async_copy(out_grad, out_grad_out, store_sem.at[2])
    grad_store.start()

    across = score_grad[...].T[:16, :]
    part0 = across.astype(BF16)
    rest = across - part0.astype(F32)
    part1 = rest.astype(BF16)
    part2 = (rest - part1.astype(F32)).astype(BF16)
    for s in range(STEPS):
        x = rows[:, s * chunk : (s + 1) * chunk]
        value = dot(part0, x) + (dot(part1, x) + dot(part2, x))
        router_grad[:, s * chunk : (s + 1) * chunk] = value[:1, :]

    send_home(STEPS - 1)

    def home(s, carry):
        chips_done(ret, s, ra_recv)
        return carry

    lax.fori_loop(0, STEPS, home, 0)
    ret_store = pltpu.make_async_copy(ret, ret_out, store_sem.at[3])
    ret_store.start()

    def drain_out(s, carry):
        chips_done(stage_a, s, a_send)
        nodes_done(stage_b, s, b_send)
        return carry

    def drain_back(s, carry):
        nodes_done(back, s, rb_send)
        chips_done(back_stage, s, ra_send)
        return carry

    lax.fori_loop(0, 2 * STEPS, drain_out, 0)
    lax.fori_loop(0, STEPS, drain_back, 0)
    scatter_store.wait()
    hidden_store.wait()
    grad_store.wait()
    ret_store.wait()


def finish_kernel(scatter, ret, hidden_t, out_grad, token_grad, down_grad, token_buf, down_buf, sem):
    ff = hidden_t.shape[0]
    step = 128

    def one(i, carry):
        part = pl.ds(pl.multiple_of(i * step, step), step)
        down_buf[part, :] = dot(hidden_t[part, :], out_grad[...]).astype(BF16)
        pltpu.make_async_copy(down_buf.at[part, :], down_grad.at[part, :], sem.at[0]).start()
        return carry

    lax.fori_loop(0, ff // step, one, 0)
    token_buf[...] = dot(scatter[...], ret[...]).astype(BF16)
    store = pltpu.make_async_copy(token_buf, token_grad, sem.at[1])
    store.start()
    pltpu.make_async_copy(down_buf, down_grad, sem.at[0]).wait()
    store.wait()


def local(n_node, n_chip, tokens, cotangent, chosen, group, router, w_gate, w_up, w_down):
    row_count, width = tokens.shape
    ff = w_gate.shape[2]
    cap = chosen.shape[1]
    dense = n_node * BLOCK
    packed = n_chip * BLOCK
    vmem = pl.BlockSpec(memory_space=pltpu.VMEM)
    hbm = pl.BlockSpec(memory_space=pl.ANY)
    dma = pltpu.SemaphoreType.DMA
    ret, scatter, hidden_t, out_grad, router_grad = pl.pallas_call(
        functools.partial(exchange_kernel, n_node, n_chip),
        out_shape=[
            jax.ShapeDtypeStruct((packed, width), BF16),
            jax.ShapeDtypeStruct((row_count, packed), BF16),
            jax.ShapeDtypeStruct((ff, dense), BF16),
            jax.ShapeDtypeStruct((dense, width), BF16),
            jax.ShapeDtypeStruct((1, width), F32),
        ],
        in_specs=[vmem] * 3 + [hbm] * 5,
        out_specs=[hbm] * 4 + [vmem],
        scratch_shapes=[
            pltpu.VMEM((row_count, 2 * width), BF16),
            pltpu.VMEM((width, ff), BF16),
            pltpu.VMEM((width, ff), BF16),
            pltpu.VMEM((ff, width), BF16),
            pltpu.VMEM((8, cap), jnp.int32),
            pltpu.VMEM((8 * n_node, cap), jnp.int32),
            pltpu.VMEM((dense, packed), BF16),
            pltpu.VMEM((packed, dense), BF16),
            pltpu.VMEM((packed, row_count), BF16),
            pltpu.VMEM((packed, row_count), BF16),
            pltpu.VMEM((packed, 2 * width), BF16),
            pltpu.VMEM((packed, 2 * width), BF16),
            pltpu.VMEM((dense, 2 * width), BF16),
            pltpu.VMEM((dense, 2 * width), BF16),
            pltpu.VMEM((dense, ff), F32),
            pltpu.VMEM((dense, ff), F32),
            pltpu.VMEM((dense, ff), F32),
            pltpu.VMEM((dense, 128), F32),
            pltpu.VMEM((dense, ff), BF16),
            pltpu.VMEM((ff, dense), BF16),
            pltpu.VMEM((dense, ff), BF16),
            pltpu.VMEM((dense, ff), BF16),
            pltpu.VMEM((dense, 128), F32),
            pltpu.VMEM((dense, width), BF16),
            pltpu.VMEM((dense, width), BF16),
            pltpu.VMEM((dense, width), BF16),
            pltpu.VMEM((packed, width), BF16),
            pltpu.VMEM((packed, width), BF16),
            pltpu.VMEM((row_count, packed), BF16),
            dma((5,)),
            dma((4,)),
            dma((2,)),
            dma((2,)),
            dma((2 * STEPS,)),
            dma((2 * STEPS,)),
            dma((2 * STEPS,)),
            dma((2 * STEPS,)),
            dma((STEPS,)),
            dma((STEPS,)),
            dma((STEPS,)),
            dma((STEPS,)),
        ],
        compiler_params=pltpu.CompilerParams(
            collective_id=0, has_side_effects=True, vmem_limit_bytes=56 * 1024 * 1024
        ),
        name="exchange",
    )(
        chosen,
        group.reshape(1, 1),
        router,
        tokens,
        cotangent,
        w_gate[0],
        w_up[0],
        w_down[0],
    )
    token_grad, down_grad = pl.pallas_call(
        finish_kernel,
        out_shape=[
            jax.ShapeDtypeStruct((row_count, width), BF16),
            jax.ShapeDtypeStruct((ff, width), BF16),
        ],
        in_specs=[vmem] * 4,
        out_specs=[hbm] * 2,
        scratch_shapes=[
            pltpu.VMEM((row_count, width), BF16),
            pltpu.VMEM((ff, width), BF16),
            dma((2,)),
        ],
        compiler_params=pltpu.CompilerParams(vmem_limit_bytes=32 * 1024 * 1024),
        name="finish",
    )(scatter, ret, hidden_t, out_grad)
    return token_grad, down_grad[None], router_grad


def solution(mesh):
    rows = P(("node", "chip"), None)
    weight = P(("node", "chip"), None, None)
    return jax.shard_map(
        functools.partial(local, mesh.shape["node"], mesh.shape["chip"]),
        mesh=mesh,
        in_specs=(rows, rows, rows, P(("node", "chip")), rows, weight, weight, weight),
        out_specs=(rows, weight, rows),
        check_vma=False,
    )
```

```python
import functools

import jax
import jax.numpy as jnp
from jax import lax
from jax.experimental import pallas as pl
from jax.experimental.pallas import tpu as pltpu
from jax.sharding import PartitionSpec as P

MESH = pl.DeviceIdType.MESH
F32 = jnp.float32
BF16 = jnp.bfloat16
BLOCK = 16
STEPS = 4
LEAD = 2
LAG = 3


def dot(a, b):
    return jnp.dot(a, b, preferred_element_type=F32)


def dot_nt(a, b):
    return lax.dot_general(a, b, (((1,), (1,)), ((), ())), preferred_element_type=F32)


def exchange_kernel(
    n_node,
    n_chip,
    chosen_hbm,
    group,
    router_hbm,
    tokens,
    cotangent,
    w_gate_hbm,
    w_up_hbm,
    w_down_hbm,
    ret_out,
    scatter_out,
    hidden_t_out,
    out_grad_out,
    router_grad_out,
    chosen,
    router,
    both,
    w_gate,
    w_up,
    w_down,
    list_send,
    lists,
    expand,
    compact,
    pick_send,
    pick_mine,
    stage_a,
    mid,
    stage_b,
    rows,
    pre_gate,
    pre_up,
    raw,
    score,
    hidden,
    hidden_t,
    gate_grad,
    up_grad,
    score_grad,
    out_grad,
    back,
    back_mid,
    back_stage,
    ret,
    scatter,
    router_grad,
    load_sem,
    store_sem,
    list_sem,
    pick_sem,
    a_send,
    a_recv,
    b_send,
    b_recv,
    rb_send,
    rb_recv,
    ra_send,
    ra_recv,
):
    n = lax.axis_index("node")
    c = lax.axis_index("chip")
    width = router.shape[1]
    ff = w_gate.shape[1]
    chunk = width // STEPS
    dense = n_node * BLOCK
    packed = n_chip * BLOCK

    small_loads = [
        pltpu.make_async_copy(chosen_hbm, chosen, load_sem.at[5]),
        pltpu.make_async_copy(router_hbm, router, load_sem.at[6]),
    ]
    for load in small_loads:
        load.start()
    loads = [
        pltpu.make_async_copy(tokens, both.at[:, pl.ds(0, width)], load_sem.at[0]),
        pltpu.make_async_copy(cotangent, both.at[:, pl.ds(width, width)], load_sem.at[1]),
        pltpu.make_async_copy(w_gate_hbm, w_gate, load_sem.at[2]),
        pltpu.make_async_copy(w_up_hbm, w_up, load_sem.at[3]),
        pltpu.make_async_copy(w_down_hbm, w_down, load_sem.at[4]),
    ]
    for load in loads:
        load.start()

    def node_peer(i):
        return lax.rem(n + i, n_node)

    def chip_peer(i):
        return lax.rem(c + i, n_chip)

    barrier = pltpu.get_barrier_semaphore()

    def greet_node(i, carry):
        pl.semaphore_signal(barrier, inc=1, device_id=(node_peer(i), c), device_id_type=MESH)
        return carry

    def greet_chip(i, carry):
        pl.semaphore_signal(barrier, inc=1, device_id=(n, chip_peer(i)), device_id_type=MESH)
        return carry

    lax.fori_loop(1, n_node, greet_node, 0)
    lax.fori_loop(1, n_chip, greet_chip, 0)

    for load in small_loads:
        load.wait()
    cap = chosen.shape[1]
    slot_index = lax.broadcasted_iota(jnp.int32, (8, cap), 1)
    live = jnp.right_shift(jnp.full((8, cap), cap, jnp.int32), jnp.broadcast_to(group[...], (8, cap)))
    own_list = jnp.where(slot_index < live, jnp.broadcast_to(chosen[...], (8, cap)), -1)
    list_send[...] = own_list
    lists[pl.ds(pl.multiple_of(n * 8, 8), 8), :] = own_list

    pl.semaphore_wait(barrier, n_node + n_chip - 2)

    def send_list(i, carry):
        pltpu.make_async_remote_copy(
            src_ref=list_send,
            dst_ref=lists.at[pl.ds(pl.multiple_of(n * 8, 8), 8), :],
            send_sem=list_sem.at[0],
            recv_sem=list_sem.at[1],
            device_id=(node_peer(i), c),
            device_id_type=MESH,
        ).start()
        return carry

    lax.fori_loop(1, n_node, send_list, 0)

    pre_gate[...] = jnp.zeros_like(pre_gate)
    pre_up[...] = jnp.zeros_like(pre_up)
    raw[...] = jnp.zeros_like(raw)
    score[...] = jnp.zeros_like(score)

    def wait_bytes(ref, sem):
        pltpu.make_async_copy(ref, ref, sem).wait()

    wait_bytes(lists.at[pl.ds(0, (n_node - 1) * 8), :], list_sem.at[0])
    wait_bytes(lists.at[pl.ds(0, (n_node - 1) * 8), :], list_sem.at[1])

    source = lax.broadcasted_iota(jnp.int32, (8, 1), 0)
    lane_row = lax.broadcasted_iota(jnp.int32, (8, cap), 1)
    lane_slot = lax.broadcasted_iota(jnp.int32, (8, packed), 1)
    used = jnp.zeros((8, 1), jnp.int32)
    expand_parts, row_parts = [], []
    for e in range(n_node):
        listed = lists[8 * e : 8 * e + 8, :]
        mine = jnp.right_shift(listed, 8) == n * n_chip + source
        local_row = jnp.bitwise_and(listed, 255)
        low = jnp.min(jnp.where(mine, local_row, 256), axis=1, keepdims=True)
        high = jnp.max(jnp.where(mine, local_row, -1), axis=1, keepdims=True)
        place = source * BLOCK + used
        first = jnp.where(high >= 0, place, -1)
        second = jnp.where(high > low, place + 8, -1)
        expand_parts.append(jnp.where(lane_slot == first, 1.0, 0.0))
        expand_parts.append(jnp.where(lane_slot == second, 1.0, 0.0))
        row_parts.append(jnp.where(lane_row == low, 1.0, 0.0))
        row_parts.append(jnp.where(lane_row == high, 1.0, 0.0))
        used = used + jnp.where(high >= 0, 1, 0)
    expand_f32 = jnp.concatenate(expand_parts, axis=0)
    expand[...] = expand_f32.astype(BF16)
    compact[...] = expand_f32.T.astype(BF16)
    row_hot = jnp.concatenate(row_parts, axis=0).astype(BF16)
    pick_send[...] = dot(compact[...], row_hot).astype(BF16)

    def block(i):
        return pl.ds(pl.multiple_of(i * BLOCK, BLOCK), BLOCK)

    def send_pick(i, carry):
        to = chip_peer(i)
        pltpu.make_async_remote_copy(
            src_ref=pick_send.at[block(to), :],
            dst_ref=pick_mine.at[block(c), :],
            send_sem=pick_sem.at[0],
            recv_sem=pick_sem.at[1],
            device_id=(n, to),
            device_id_type=MESH,
        ).start()
        return carry

    lax.fori_loop(1, n_chip, send_pick, 0)
    pick_mine[block(c), :] = pick_send[block(c), :]
    loads[0].wait()
    loads[1].wait()
    wait_bytes(pick_mine.at[pl.ds(0, (n_chip - 1) * BLOCK), :], pick_sem.at[0])
    wait_bytes(pick_mine.at[pl.ds(0, (n_chip - 1) * BLOCK), :], pick_sem.at[1])

    def cols(s):
        return pl.ds(pl.multiple_of(s * chunk, chunk), chunk)

    def to_chips(src, dst, s, send_sem, recv_sem):
        def one(i, carry):
            to = chip_peer(i)
            pltpu.make_async_remote_copy(
                src_ref=src.at[block(to), cols(s)],
                dst_ref=dst.at[block(c), cols(s)],
                send_sem=send_sem.at[s],
                recv_sem=recv_sem.at[s],
                device_id=(n, to),
                device_id_type=MESH,
            ).start()
            return carry

        lax.fori_loop(1, n_chip, one, 0)
        dst[block(c), cols(s)] = src[block(c), cols(s)]

    def to_nodes(src, dst, s, send_sem, recv_sem):
        def one(i, carry):
            to = node_peer(i)
            pltpu.make_async_remote_copy(
                src_ref=src.at[block(to), cols(s)],
                dst_ref=dst.at[block(n), cols(s)],
                send_sem=send_sem.at[s],
                recv_sem=recv_sem.at[s],
                device_id=(to, c),
                device_id_type=MESH,
            ).start()
            return carry

        lax.fori_loop(1, n_node, one, 0)
        dst[block(n), cols(s)] = src[block(n), cols(s)]

    def chips_done(ref, s, sem):
        wait_bytes(ref.at[pl.ds(0, packed - BLOCK), cols(s)], sem.at[s])

    def nodes_done(ref, s, sem):
        wait_bytes(ref.at[pl.ds(0, dense - BLOCK), cols(s)], sem.at[s])

    def gather(s):
        stage_a[:, cols(s)] = dot(pick_mine[...], both[:, cols(s)]).astype(BF16)
        to_chips(stage_a, mid, s, a_send, a_recv)

    def forward(s):
        chips_done(mid, s, a_recv)
        stage_b[:, cols(s)] = dot(expand[...], mid[:, cols(s)]).astype(BF16)
        to_nodes(stage_b, rows, s, b_send, b_recv)

    def up_step(s):
        nodes_done(rows, s, b_recv)
        x = rows[:, cols(s)]
        pre_gate[...] += dot(x, w_gate[cols(s), :])
        pre_up[...] += dot(x, w_up[cols(s), :])
        score[...] += dot_nt(x, jnp.broadcast_to(router[:, cols(s)], (128, chunk)))

    def down_step(s):
        nodes_done(rows, s, b_recv)
        raw[...] += dot_nt(rows[:, cols(s)], w_down[:, cols(s - STEPS)])

    def from_x(r, carry):
        part = pl.ds(pl.multiple_of(r * 64, 64), 64)
        s = jax.nn.sigmoid(score[part, :])
        score[part, :] = s
        for j in range(ff // 128):
            lanes = pl.ds(128 * j, 128)
            g = pre_gate[part, lanes]
            u = pre_up[part, lanes]
            sig = jax.nn.sigmoid(g)
            act = g * sig
            hidden[part, lanes] = (act * u).astype(BF16)
            pre_gate[part, lanes] = s * (u * sig * (1.0 + g * (1.0 - sig)))
            pre_up[part, lanes] = s * act
        return carry

    for s in range(LEAD):
        gather(s)
    scatter[...] = pick_mine[...].astype(F32).T.astype(BF16)
    scatter_store = pltpu.make_async_copy(scatter, scatter_out, store_sem.at[0])
    scatter_store.start()

    def phase(t, carry):
        @pl.when(t + LEAD < 2 * STEPS)
        def _():
            gather(t + LEAD)

        @pl.when(t < 2 * STEPS)
        def _():
            forward(t)

        @pl.when(t == LAG)
        def _():
            loads[2].wait()
            loads[3].wait()

        @pl.when((t >= LAG) & (t < STEPS + LAG))
        def _():
            up_step(t - LAG)

        @pl.when(t == STEPS + LAG)
        def _():
            lax.fori_loop(0, dense // 64, from_x, 0)
            loads[4].wait()

        @pl.when(t >= STEPS + LAG)
        def _():
            down_step(t - LAG)

        return carry

    lax.fori_loop(0, 2 * STEPS + LAG, phase, 0)

    def from_dy(r, carry):
        part = pl.ds(pl.multiple_of(r * 64, 64), 64)
        total = jnp.zeros((64, 128), F32)
        for j in range(ff // 128):
            lanes = pl.ds(128 * j, 128)
            v = raw[part, lanes]
            total = total + v * hidden[part, lanes].astype(F32)
            gate_grad[part, lanes] = (v * pre_gate[part, lanes]).astype(BF16)
            up_grad[part, lanes] = (v * pre_up[part, lanes]).astype(BF16)
        s = score[part, :]
        score_grad[part, :] = jnp.sum(total, axis=1, keepdims=True) * s * (1.0 - s)
        return carry

    lax.fori_loop(0, dense // 64, from_dy, 0)

    def send_back(s):
        value = dot_nt(gate_grad[...], w_gate[cols(s), :])
        value = value + dot_nt(up_grad[...], w_up[cols(s), :])
        value = value + score_grad[:, :1] * router[:, cols(s)].astype(F32)
        back[:, cols(s)] = value.astype(BF16)
        to_nodes(back, back_mid, s, rb_send, rb_recv)

    def send_home(s):
        nodes_done(back_mid, s, rb_recv)
        back_stage[:, cols(s)] = dot(compact[...], back_mid[:, cols(s)]).astype(BF16)
        to_chips(back_stage, ret, s, ra_send, ra_recv)

    def return_phase(s, carry):
        send_back(s)
        return carry

    lax.fori_loop(0, STEPS, return_phase, 0)
    hidden_t[...] = hidden[...].astype(F32).T.astype(BF16)
    hidden_store = pltpu.make_async_copy(hidden_t, hidden_t_out, store_sem.at[1])
    hidden_store.start()

    def scale(r, carry):
        part = pl.ds(pl.multiple_of(r * 16, 16), 16)
        s = score[part, :1]
        out_grad[part, :] = (s * rows[part, width:].astype(F32)).astype(BF16)
        return carry

    lax.fori_loop(0, dense // 16, scale, 0)
    grad_store = pltpu.make_async_copy(out_grad, out_grad_out, store_sem.at[2])
    grad_store.start()

    across = score_grad[...].T[:16, :]
    part0 = across.astype(BF16)
    rest = across - part0.astype(F32)
    part1 = rest.astype(BF16)
    part2 = (rest - part1.astype(F32)).astype(BF16)
    for s in range(STEPS):
        x = rows[:, s * chunk : (s + 1) * chunk]
        value = dot(part0, x) + (dot(part1, x) + dot(part2, x))
        router_grad[:, s * chunk : (s + 1) * chunk] = value[:1, :]

    router_store = pltpu.make_async_copy(router_grad, router_grad_out, store_sem.at[4])
    router_store.start()

    def home_phase(s, carry):
        send_home(s)
        return carry

    lax.fori_loop(0, STEPS, home_phase, 0)

    def home(s, carry):
        chips_done(ret, s, ra_recv)
        return carry

    lax.fori_loop(0, STEPS, home, 0)
    ret_store = pltpu.make_async_copy(ret, ret_out, store_sem.at[3])
    ret_store.start()

    def drain_out(s, carry):
        chips_done(stage_a, s, a_send)
        nodes_done(stage_b, s, b_send)
        return carry

    def drain_back(s, carry):
        nodes_done(back, s, rb_send)
        chips_done(back_stage, s, ra_send)
        return carry

    lax.fori_loop(0, 2 * STEPS, drain_out, 0)
    lax.fori_loop(0, STEPS, drain_back, 0)
    scatter_store.wait()
    hidden_store.wait()
    grad_store.wait()
    router_store.wait()
    ret_store.wait()


def finish_kernel(
    scatter_hbm,
    ret_hbm,
    hidden_t_hbm,
    out_grad_hbm,
    router_grad_hbm,
    token_grad,
    down_grad,
    router_grad,
    scatter,
    ret,
    hidden_t,
    out_grad,
    token_buf,
    down_buf,
    load_sem,
    store_sem,
):
    ff = hidden_t.shape[0]
    parts = 4
    step = ff // parts
    pass_on = pltpu.make_async_copy(router_grad_hbm, router_grad, store_sem.at[2])
    loads = [
        pltpu.make_async_copy(out_grad_hbm, out_grad, load_sem.at[0]),
        pltpu.make_async_copy(hidden_t_hbm, hidden_t, load_sem.at[1]),
        pltpu.make_async_copy(ret_hbm, ret, load_sem.at[2]),
        pltpu.make_async_copy(scatter_hbm, scatter, load_sem.at[3]),
    ]
    for load in loads:
        load.start()
    pass_on.start()
    loads[0].wait()
    loads[1].wait()

    def one(i, carry):
        part = pl.ds(pl.multiple_of(i * step, 32), step)
        down_buf[part, :] = dot(hidden_t[part, :], out_grad[...]).astype(BF16)
        pltpu.make_async_copy(down_buf.at[part, :], down_grad.at[part, :], store_sem.at[0]).start()
        return carry

    lax.fori_loop(0, parts, one, 0)
    loads[2].wait()
    loads[3].wait()
    token_buf[...] = dot(scatter[...], ret[...]).astype(BF16)
    store = pltpu.make_async_copy(token_buf, token_grad, store_sem.at[1])
    store.start()
    pltpu.make_async_copy(down_buf, down_grad, store_sem.at[0]).wait()
    store.wait()
    pass_on.wait()


def local(n_node, n_chip, tokens, cotangent, chosen, group, router, w_gate, w_up, w_down):
    row_count, width = tokens.shape
    ff = w_gate.shape[2]
    cap = chosen.shape[1]
    dense = n_node * BLOCK
    packed = n_chip * BLOCK
    vmem = pl.BlockSpec(memory_space=pltpu.VMEM)
    hbm = pl.BlockSpec(memory_space=pl.ANY)
    dma = pltpu.SemaphoreType.DMA
    ret, scatter, hidden_t, out_grad, router_grad = pl.pallas_call(
        functools.partial(exchange_kernel, n_node, n_chip),
        out_shape=[
            jax.ShapeDtypeStruct((packed, width), BF16),
            jax.ShapeDtypeStruct((row_count, packed), BF16),
            jax.ShapeDtypeStruct((ff, dense), BF16),
            jax.ShapeDtypeStruct((dense, width), BF16),
            jax.ShapeDtypeStruct((1, width), F32),
        ],
        in_specs=[hbm, vmem] + [hbm] * 6,
        out_specs=[hbm] * 5,
        scratch_shapes=[
            pltpu.VMEM((1, cap), jnp.int32),
            pltpu.VMEM((1, width), BF16),
            pltpu.VMEM((row_count, 2 * width), BF16),
            pltpu.VMEM((width, ff), BF16),
            pltpu.VMEM((width, ff), BF16),
            pltpu.VMEM((ff, width), BF16),
            pltpu.VMEM((8, cap), jnp.int32),
            pltpu.VMEM((8 * n_node, cap), jnp.int32),
            pltpu.VMEM((dense, packed), BF16),
            pltpu.VMEM((packed, dense), BF16),
            pltpu.VMEM((packed, row_count), BF16),
            pltpu.VMEM((packed, row_count), BF16),
            pltpu.VMEM((packed, 2 * width), BF16),
            pltpu.VMEM((packed, 2 * width), BF16),
            pltpu.VMEM((dense, 2 * width), BF16),
            pltpu.VMEM((dense, 2 * width), BF16),
            pltpu.VMEM((dense, ff), F32),
            pltpu.VMEM((dense, ff), F32),
            pltpu.VMEM((dense, ff), F32),
            pltpu.VMEM((dense, 128), F32),
            pltpu.VMEM((dense, ff), BF16),
            pltpu.VMEM((ff, dense), BF16),
            pltpu.VMEM((dense, ff), BF16),
            pltpu.VMEM((dense, ff), BF16),
            pltpu.VMEM((dense, 128), F32),
            pltpu.VMEM((dense, width), BF16),
            pltpu.VMEM((dense, width), BF16),
            pltpu.VMEM((dense, width), BF16),
            pltpu.VMEM((packed, width), BF16),
            pltpu.VMEM((packed, width), BF16),
            pltpu.VMEM((row_count, packed), BF16),
            pltpu.VMEM((1, width), F32),
            dma((7,)),
            dma((5,)),
            dma((2,)),
            dma((2,)),
            dma((2 * STEPS,)),
            dma((2 * STEPS,)),
            dma((2 * STEPS,)),
            dma((2 * STEPS,)),
            dma((STEPS,)),
            dma((STEPS,)),
            dma((STEPS,)),
            dma((STEPS,)),
        ],
        compiler_params=pltpu.CompilerParams(
            collective_id=0, has_side_effects=True, vmem_limit_bytes=58 * 1024 * 1024
        ),
        name="exchange",
    )(
        chosen,
        group.reshape(1, 1),
        router,
        tokens,
        cotangent,
        w_gate[0],
        w_up[0],
        w_down[0],
    )
    token_grad, down_grad, router_grad = pl.pallas_call(
        finish_kernel,
        out_shape=[
            jax.ShapeDtypeStruct((row_count, width), BF16),
            jax.ShapeDtypeStruct((ff, width), BF16),
            jax.ShapeDtypeStruct((1, width), F32),
        ],
        in_specs=[hbm] * 5,
        out_specs=[hbm] * 3,
        scratch_shapes=[
            pltpu.VMEM((row_count, packed), BF16),
            pltpu.VMEM((packed, width), BF16),
            pltpu.VMEM((ff, dense), BF16),
            pltpu.VMEM((dense, width), BF16),
            pltpu.VMEM((row_count, width), BF16),
            pltpu.VMEM((ff, width), BF16),
            dma((4,)),
            dma((3,)),
        ],
        compiler_params=pltpu.CompilerParams(vmem_limit_bytes=58 * 1024 * 1024),
        name="finish",
    )(scatter, ret, hidden_t, out_grad, router_grad)
    return token_grad, down_grad[None], router_grad


def solution(mesh):
    rows = P(("node", "chip"), None)
    weight = P(("node", "chip"), None, None)
    return jax.shard_map(
        functools.partial(local, mesh.shape["node"], mesh.shape["chip"]),
        mesh=mesh,
        in_specs=(rows, rows, rows, P(("node", "chip")), rows, weight, weight, weight),
        out_specs=(rows, weight, rows),
        check_vma=False,
    )
```

```python
import functools

import jax
import jax.numpy as jnp
from jax import lax
from jax.experimental import pallas as pl
from jax.experimental.pallas import tpu as pltpu
from jax.sharding import PartitionSpec as P

MESH = pl.DeviceIdType.MESH
F32 = jnp.float32
BF16 = jnp.bfloat16
NODE_STEPS = (
    (2, 2), (3, 2), (2, 3), (1, 2), (2, 1), (0, 2), (2, 0),
    (3, 1), (1, 3), (3, 3), (1, 1), (0, 3), (3, 0), (0, 1), (1, 0),
)
CHIP_STEPS = (5, 4, 3, 2, 7, 6, 1)
BLOCK = 16
STEPS = 4
LEAD = 2
LAG = 3


def dot(a, b):
    return jnp.dot(a, b, preferred_element_type=F32)


def dot_nt(a, b):
    return lax.dot_general(a, b, (((1,), (1,)), ((), ())), preferred_element_type=F32)


def exchange_kernel(
    n_node,
    n_chip,
    chosen_hbm,
    group,
    router_hbm,
    tokens,
    cotangent,
    w_gate_hbm,
    w_up_hbm,
    w_down_hbm,
    token_grad,
    down_grad,
    router_grad,
    chosen,
    router,
    both,
    w_gate,
    w_up,
    w_down,
    list_send,
    lists,
    expand,
    compact,
    pick_send,
    pick_mine,
    stage_a,
    mid,
    stage_b,
    rows,
    pre_gate,
    pre_up,
    raw,
    score,
    hidden,
    hidden_t,
    gate_grad,
    up_grad,
    score_grad,
    out_grad,
    back,
    back_mid,
    back_stage,
    ret,
    scatter,
    load_sem,
    list_sem,
    pick_sem,
    a_send,
    a_recv,
    b_send,
    b_recv,
    rb_send,
    rb_recv,
    ra_send,
    ra_recv,
):
    n = lax.axis_index("node")
    c = lax.axis_index("chip")
    width = router.shape[1]
    ff = w_gate.shape[1]
    chunk = width // STEPS
    dense = n_node * BLOCK
    packed = n_chip * BLOCK

    small_loads = [
        pltpu.make_async_copy(chosen_hbm, chosen, load_sem.at[5]),
        pltpu.make_async_copy(router_hbm, router, load_sem.at[6]),
    ]
    for load in small_loads:
        load.start()
    loads = [
        pltpu.make_async_copy(tokens, both.at[:, pl.ds(0, width)], load_sem.at[0]),
        pltpu.make_async_copy(cotangent, both.at[:, pl.ds(width, width)], load_sem.at[1]),
        pltpu.make_async_copy(w_gate_hbm, w_gate, load_sem.at[2]),
        pltpu.make_async_copy(w_up_hbm, w_up, load_sem.at[3]),
        pltpu.make_async_copy(w_down_hbm, w_down, load_sem.at[4]),
    ]
    for load in loads:
        load.start()

    def node_peer(step):
        y, z = step
        return lax.rem(n // 4 + y, 4) * 4 + lax.rem(lax.rem(n, 4) + z, 4)

    def chip_peer(i):
        return lax.rem(c + i, n_chip)

    barrier = pltpu.get_barrier_semaphore()

    for step in NODE_STEPS:
        pl.semaphore_signal(barrier, inc=1, device_id=(node_peer(step), c), device_id_type=MESH)
    for step in CHIP_STEPS:
        pl.semaphore_signal(barrier, inc=1, device_id=(n, chip_peer(step)), device_id_type=MESH)

    for load in small_loads:
        load.wait()
    cap = chosen.shape[1]
    slot_index = lax.broadcasted_iota(jnp.int32, (1, cap), 1)
    live = jnp.right_shift(jnp.full((1, cap), cap, jnp.int32), jnp.broadcast_to(group[...], (1, cap)))
    own_list = jnp.where(slot_index < live, chosen[...], -1)
    list_send[...] = own_list
    lists[n] = own_list

    pl.semaphore_wait(barrier, n_node + n_chip - 2)

    for step in NODE_STEPS:
        pltpu.make_async_remote_copy(
            src_ref=list_send,
            dst_ref=lists.at[n],
            send_sem=list_sem.at[0],
            recv_sem=list_sem.at[1],
            device_id=(node_peer(step), c),
            device_id_type=MESH,
        ).start()

    pre_gate[...] = jnp.zeros_like(pre_gate)
    pre_up[...] = jnp.zeros_like(pre_up)
    raw[...] = jnp.zeros_like(raw)
    score[...] = jnp.zeros_like(score)

    def wait_bytes(ref, sem):
        pltpu.make_async_copy(ref, ref, sem).wait()

    wait_bytes(lists.at[pl.ds(0, n_node - 1)], list_sem.at[1])

    source = lax.broadcasted_iota(jnp.int32, (8, 1), 0)
    lane_row = lax.broadcasted_iota(jnp.int32, (8, cap), 1)
    lane_slot = lax.broadcasted_iota(jnp.int32, (8, packed), 1)
    used = jnp.zeros((8, 1), jnp.int32)
    expand_parts, row_parts = [], []
    for e in range(n_node):
        listed = jnp.broadcast_to(lists[e], (8, cap))
        mine = jnp.right_shift(listed, 8) == n * n_chip + source
        local_row = jnp.bitwise_and(listed, 255)
        low = jnp.min(jnp.where(mine, local_row, 256), axis=1, keepdims=True)
        high = jnp.max(jnp.where(mine, local_row, -1), axis=1, keepdims=True)
        place = source * BLOCK + used
        first = jnp.where(high >= 0, place, -1)
        second = jnp.where(high > low, place + 8, -1)
        expand_parts.append(jnp.where(lane_slot == first, 1.0, 0.0))
        expand_parts.append(jnp.where(lane_slot == second, 1.0, 0.0))
        row_parts.append(jnp.where(lane_row == low, 1.0, 0.0))
        row_parts.append(jnp.where(lane_row == high, 1.0, 0.0))
        used = used + jnp.where(high >= 0, 1, 0)
    expand_f32 = jnp.concatenate(expand_parts, axis=0)
    expand[...] = expand_f32.astype(BF16)
    compact[...] = expand_f32.T.astype(BF16)
    row_hot = jnp.concatenate(row_parts, axis=0).astype(BF16)
    pick_send[...] = dot(compact[...], row_hot).astype(BF16)

    def block(i):
        return pl.ds(pl.multiple_of(i * BLOCK, BLOCK), BLOCK)

    for step in CHIP_STEPS:
        to = chip_peer(step)
        pltpu.make_async_remote_copy(
            src_ref=pick_send.at[block(to), :],
            dst_ref=pick_mine.at[block(c), :],
            send_sem=pick_sem.at[0],
            recv_sem=pick_sem.at[1],
            device_id=(n, to),
            device_id_type=MESH,
        ).start()
    pick_mine[block(c), :] = pick_send[block(c), :]
    loads[0].wait()
    loads[1].wait()
    wait_bytes(pick_mine.at[pl.ds(0, (n_chip - 1) * BLOCK), :], pick_sem.at[1])

    def cols(s):
        return pl.ds(pl.multiple_of(s * chunk, chunk), chunk)

    def to_chips(src, dst, s, send_sem, recv_sem):
        for step in CHIP_STEPS:
            to = chip_peer(step)
            pltpu.make_async_remote_copy(
                src_ref=src.at[block(to), cols(s)],
                dst_ref=dst.at[block(c), cols(s)],
                send_sem=send_sem.at[s],
                recv_sem=recv_sem.at[s],
                device_id=(n, to),
                device_id_type=MESH,
            ).start()
        dst[block(c), cols(s)] = src[block(c), cols(s)]

    def to_nodes(src, dst, s, send_sem, recv_sem):
        for step in NODE_STEPS:
            to = node_peer(step)
            pltpu.make_async_remote_copy(
                src_ref=src.at[block(to), cols(s)],
                dst_ref=dst.at[block(n), cols(s)],
                send_sem=send_sem.at[s],
                recv_sem=recv_sem.at[s],
                device_id=(to, c),
                device_id_type=MESH,
            ).start()
        dst[block(n), cols(s)] = src[block(n), cols(s)]

    def chips_done(ref, s, sem):
        wait_bytes(ref.at[pl.ds(0, packed - BLOCK), cols(s)], sem.at[s])

    def nodes_done(ref, s, sem):
        wait_bytes(ref.at[pl.ds(0, dense - BLOCK), cols(s)], sem.at[s])

    def gather(s):
        stage_a[:, cols(s)] = dot(pick_mine[...], both[:, cols(s)]).astype(BF16)
        to_chips(stage_a, mid, s, a_send, a_recv)

    def forward(s):
        chips_done(mid, s, a_recv)
        stage_b[:, cols(s)] = dot(expand[...], mid[:, cols(s)]).astype(BF16)
        to_nodes(stage_b, rows, s, b_send, b_recv)

    def up_step(s):
        nodes_done(rows, s, b_recv)
        x = rows[:, cols(s)]
        pre_gate[...] += dot(x, w_gate[cols(s), :])
        pre_up[...] += dot(x, w_up[cols(s), :])
        score[...] += dot_nt(x, jnp.broadcast_to(router[:, cols(s)], (128, chunk)))

    def down_step(s):
        nodes_done(rows, s, b_recv)
        raw[...] += dot_nt(rows[:, cols(s)], w_down[:, cols(s - STEPS)])

    def from_x(r, carry):
        part = pl.ds(pl.multiple_of(r * 64, 64), 64)
        s = jax.nn.sigmoid(score[part, :])
        score[part, :] = s
        for j in range(ff // 128):
            lanes = pl.ds(128 * j, 128)
            g = pre_gate[part, lanes]
            u = pre_up[part, lanes]
            sig = jax.nn.sigmoid(g)
            act = g * sig
            hidden[part, lanes] = (act * u).astype(BF16)
            pre_gate[part, lanes] = s * (u * sig * (1.0 + g * (1.0 - sig)))
            pre_up[part, lanes] = s * act
        return carry

    for s in range(LEAD):
        gather(s)
    scatter[...] = pick_mine[...].astype(F32).T.astype(BF16)

    def phase(t, carry):
        @pl.when(t + LEAD < 2 * STEPS)
        def _():
            gather(t + LEAD)

        @pl.when(t < 2 * STEPS)
        def _():
            forward(t)

        @pl.when(t == LAG)
        def _():
            loads[2].wait()
            loads[3].wait()

        @pl.when((t >= LAG) & (t < STEPS + LAG))
        def _():
            up_step(t - LAG)

        @pl.when(t == STEPS + LAG)
        def _():
            lax.fori_loop(0, dense // 64, from_x, 0)
            loads[4].wait()

        @pl.when(t >= STEPS + LAG)
        def _():
            down_step(t - LAG)

        return carry

    lax.fori_loop(0, 2 * STEPS + LAG, phase, 0)

    def from_dy(r, carry):
        part = pl.ds(pl.multiple_of(r * 64, 64), 64)
        total = jnp.zeros((64, 128), F32)
        for j in range(ff // 128):
            lanes = pl.ds(128 * j, 128)
            v = raw[part, lanes]
            total = total + v * hidden[part, lanes].astype(F32)
            gate_grad[part, lanes] = (v * pre_gate[part, lanes]).astype(BF16)
            up_grad[part, lanes] = (v * pre_up[part, lanes]).astype(BF16)
        s = score[part, :]
        score_grad[part, :] = jnp.sum(total, axis=1, keepdims=True) * s * (1.0 - s)
        return carry

    lax.fori_loop(0, dense // 64, from_dy, 0)

    def send_back(s):
        value = dot_nt(gate_grad[...], w_gate[cols(s), :])
        value = value + dot_nt(up_grad[...], w_up[cols(s), :])
        value = value + score_grad[:, :1] * router[:, cols(s)].astype(F32)
        back[:, cols(s)] = value.astype(BF16)
        to_nodes(back, back_mid, s, rb_send, rb_recv)

    def send_home(s):
        nodes_done(back_mid, s, rb_recv)
        back_stage[:, cols(s)] = dot(compact[...], back_mid[:, cols(s)]).astype(BF16)
        to_chips(back_stage, ret, s, ra_send, ra_recv)

    def return_phase(s, carry):
        send_back(s)
        return carry

    lax.fori_loop(0, STEPS, return_phase, 0)
    hidden_t[...] = hidden[...].astype(F32).T.astype(BF16)

    def scale(r, carry):
        part = pl.ds(pl.multiple_of(r * 16, 16), 16)
        s = score[part, :1]
        out_grad[part, :] = (s * rows[part, width:].astype(F32)).astype(BF16)
        return carry

    lax.fori_loop(0, dense // 16, scale, 0)
    def down_phase(r, carry):
        part = pl.ds(pl.multiple_of(r * (ff // 4), 32), ff // 4)
        down_grad[part, :] = dot(hidden_t[part, :], out_grad[...]).astype(BF16)
        return carry

    lax.fori_loop(0, 4, down_phase, 0)

    across = score_grad[...].T[:16, :]
    part0 = across.astype(BF16)
    rest = across - part0.astype(F32)
    part1 = rest.astype(BF16)
    part2 = (rest - part1.astype(F32)).astype(BF16)
    for s in range(STEPS):
        x = rows[:, s * chunk : (s + 1) * chunk]
        value = dot(part0, x) + (dot(part1, x) + dot(part2, x))
        router_grad[:, s * chunk : (s + 1) * chunk] = value[:1, :]

    def home_phase(s, carry):
        send_home(s)
        return carry

    lax.fori_loop(0, STEPS, home_phase, 0)

    def home(s, carry):
        chips_done(ret, s, ra_recv)
        token_grad[:, cols(s)] = dot(scatter[...], ret[:, cols(s)]).astype(BF16)
        return carry

    lax.fori_loop(0, STEPS, home, 0)
    wait_bytes(lists.at[pl.ds(0, n_node - 1)], list_sem.at[0])
    wait_bytes(pick_mine.at[pl.ds(0, (n_chip - 1) * BLOCK), :], pick_sem.at[0])

    def drain_out(s, carry):
        chips_done(stage_a, s, a_send)
        nodes_done(stage_b, s, b_send)
        return carry

    def drain_back(s, carry):
        nodes_done(back, s, rb_send)
        chips_done(back_stage, s, ra_send)
        return carry

    lax.fori_loop(0, 2 * STEPS, drain_out, 0)
    lax.fori_loop(0, STEPS, drain_back, 0)


def finish_kernel(token_in, down_in, router_in, token_grad, down_grad, router_grad, sem):
    stores = [
        pltpu.make_async_copy(down_in, down_grad, sem.at[0]),
        pltpu.make_async_copy(token_in, token_grad, sem.at[1]),
        pltpu.make_async_copy(router_in, router_grad, sem.at[2]),
    ]
    for store in stores:
        store.start()
    for store in stores:
        store.wait()


def local(n_node, n_chip, tokens, cotangent, chosen, group, router, w_gate, w_up, w_down):
    row_count, width = tokens.shape
    ff = w_gate.shape[2]
    cap = chosen.shape[1]
    dense = n_node * BLOCK
    packed = n_chip * BLOCK
    vmem = pl.BlockSpec(memory_space=pltpu.VMEM)
    hbm = pl.BlockSpec(memory_space=pl.ANY)
    dma = pltpu.SemaphoreType.DMA
    results = pl.pallas_call(
        functools.partial(exchange_kernel, n_node, n_chip),
        out_shape=[
            pltpu.VMEM((row_count, width), BF16),
            pltpu.VMEM((ff, width), BF16),
            pltpu.VMEM((1, width), F32),
        ],
        in_specs=[hbm, vmem] + [hbm] * 6,
        out_specs=[vmem] * 3,
        scratch_shapes=[
            pltpu.VMEM((1, cap), jnp.int32),
            pltpu.VMEM((1, width), BF16),
            pltpu.VMEM((row_count, 2 * width), BF16),
            pltpu.VMEM((width, ff), BF16),
            pltpu.VMEM((width, ff), BF16),
            pltpu.VMEM((ff, width), BF16),
            pltpu.VMEM((1, cap), jnp.int32),
            pltpu.VMEM((n_node, 1, cap), jnp.int32),
            pltpu.VMEM((dense, packed), BF16),
            pltpu.VMEM((packed, dense), BF16),
            pltpu.VMEM((packed, row_count), BF16),
            pltpu.VMEM((packed, row_count), BF16),
            pltpu.VMEM((packed, 2 * width), BF16),
            pltpu.VMEM((packed, 2 * width), BF16),
            pltpu.VMEM((dense, 2 * width), BF16),
            pltpu.VMEM((dense, 2 * width), BF16),
            pltpu.VMEM((dense, ff), F32),
            pltpu.VMEM((dense, ff), F32),
            pltpu.VMEM((dense, ff), F32),
            pltpu.VMEM((dense, 128), F32),
            pltpu.VMEM((dense, ff), BF16),
            pltpu.VMEM((ff, dense), BF16),
            pltpu.VMEM((dense, ff), BF16),
            pltpu.VMEM((dense, ff), BF16),
            pltpu.VMEM((dense, 128), F32),
            pltpu.VMEM((dense, width), BF16),
            pltpu.VMEM((dense, width), BF16),
            pltpu.VMEM((dense, width), BF16),
            pltpu.VMEM((packed, width), BF16),
            pltpu.VMEM((packed, width), BF16),
            pltpu.VMEM((row_count, packed), BF16),
            dma((7,)),
            dma((2,)),
            dma((2,)),
            dma((2 * STEPS,)),
            dma((2 * STEPS,)),
            dma((2 * STEPS,)),
            dma((2 * STEPS,)),
            dma((STEPS,)),
            dma((STEPS,)),
            dma((STEPS,)),
            dma((STEPS,)),
        ],
        compiler_params=pltpu.CompilerParams(
            collective_id=0, has_side_effects=True, vmem_limit_bytes=48 * 1024 * 1024
        ),
        name="exchange",
    )(
        chosen,
        group.reshape(1, 1),
        router,
        tokens,
        cotangent,
        w_gate[0],
        w_up[0],
        w_down[0],
    )
    token_grad, down_grad, router_grad = pl.pallas_call(
        finish_kernel,
        out_shape=[
            jax.ShapeDtypeStruct((row_count, width), BF16),
            jax.ShapeDtypeStruct((ff, width), BF16),
            jax.ShapeDtypeStruct((1, width), F32),
        ],
        in_specs=[vmem] * 3,
        out_specs=[hbm] * 3,
        scratch_shapes=[dma((3,))],
        compiler_params=pltpu.CompilerParams(vmem_limit_bytes=16 * 1024 * 1024),
        name="finish",
    )(*results)
    return token_grad, down_grad[None], router_grad


def solution(mesh):
    rows = P(("node", "chip"), None)
    weight = P(("node", "chip"), None, None)
    return jax.shard_map(
        functools.partial(local, mesh.shape["node"], mesh.shape["chip"]),
        mesh=mesh,
        in_specs=(rows, rows, rows, P(("node", "chip")), rows, weight, weight, weight),
        out_specs=(rows, weight, rows),
        check_vma=False,
    )
```

```python
import functools

import jax
import jax.numpy as jnp
from jax import lax
from jax.experimental import pallas as pl
from jax.experimental.pallas import tpu as pltpu
from jax.sharding import PartitionSpec as P

MESH = pl.DeviceIdType.MESH
F32 = jnp.float32
BF16 = jnp.bfloat16
NODE_STEPS = (
    (2, 2), (3, 2), (2, 3), (1, 2), (2, 1), (0, 2), (2, 0),
    (3, 1), (1, 3), (3, 3), (1, 1), (0, 3), (3, 0), (0, 1), (1, 0),
)
CHIP_STEPS = (5, 4, 3, 2, 7, 6, 1)
BLOCK = 16
STEPS = 4
FIRST = 2
LEAD = 2
LAG = 4


def dot(a, b):
    return jnp.dot(a, b, preferred_element_type=F32)


def dot_nt(a, b):
    return lax.dot_general(a, b, (((1,), (1,)), ((), ())), preferred_element_type=F32)


def exchange_kernel(
    n_node,
    n_chip,
    chosen_hbm,
    group,
    router_hbm,
    tokens,
    cotangent,
    w_gate_hbm,
    w_up_hbm,
    w_down_hbm,
    token_grad,
    down_grad,
    router_grad,
    chosen,
    router,
    both,
    w_gate,
    w_up,
    w_down,
    list_send,
    lists,
    expand,
    compact,
    pick_send,
    pick_mine,
    stage_a,
    mid,
    stage_b,
    rows,
    pre_gate,
    pre_up,
    raw,
    score,
    hidden,
    hidden_t,
    gate_grad,
    up_grad,
    score_grad,
    out_grad,
    back,
    back_mid,
    back_stage,
    ret,
    scatter,
    perm,
    perm_t,
    full_send,
    full_mine,
    full_pick,
    full_scatter,
    first_mid,
    first_turn,
    first_got,
    last_turn,
    last_mid,
    last_stage,
    last_got,
    load_sem,
    list_sem,
    pick_sem,
    full_sem,
    first_sem,
    last_sem,
    a_send,
    a_recv,
    b_send,
    b_recv,
    rb_send,
    rb_recv,
    ra_send,
    ra_recv,
):
    n = lax.axis_index("node")
    c = lax.axis_index("chip")
    width = router.shape[1]
    ff = w_gate.shape[1]
    chunk = width // STEPS
    dense = n_node * BLOCK
    packed = n_chip * BLOCK

    small_loads = [
        pltpu.make_async_copy(chosen_hbm, chosen, load_sem.at[5]),
        pltpu.make_async_copy(router_hbm, router, load_sem.at[6]),
    ]
    for load in small_loads:
        load.start()
    loads = [
        pltpu.make_async_copy(tokens, both.at[:, pl.ds(0, width)], load_sem.at[0]),
        pltpu.make_async_copy(cotangent, both.at[:, pl.ds(width, width)], load_sem.at[1]),
        pltpu.make_async_copy(w_gate_hbm, w_gate, load_sem.at[2]),
        pltpu.make_async_copy(w_up_hbm, w_up, load_sem.at[3]),
        pltpu.make_async_copy(w_down_hbm, w_down, load_sem.at[4]),
    ]
    for load in loads:
        load.start()

    def node_peer(step):
        y, z = step
        return lax.rem(n // 4 + y, 4) * 4 + lax.rem(lax.rem(n, 4) + z, 4)

    def chip_peer(i):
        return lax.rem(c + i, n_chip)

    barrier = pltpu.get_barrier_semaphore()

    for step in NODE_STEPS:
        pl.semaphore_signal(barrier, inc=1, device_id=(node_peer(step), c), device_id_type=MESH)
    for step in CHIP_STEPS:
        pl.semaphore_signal(barrier, inc=1, device_id=(n, chip_peer(step)), device_id_type=MESH)

    for load in small_loads:
        load.wait()
    cap = chosen.shape[1]
    slot_index = lax.broadcasted_iota(jnp.int32, (1, cap), 1)
    live = jnp.right_shift(jnp.full((1, cap), cap, jnp.int32), jnp.broadcast_to(group[...], (1, cap)))
    own_list = jnp.where(slot_index < live, chosen[...], -1)
    list_send[...] = own_list
    lists[n] = own_list

    pl.semaphore_wait(barrier, n_node + n_chip - 2)

    for step in NODE_STEPS:
        pltpu.make_async_remote_copy(
            src_ref=list_send,
            dst_ref=lists.at[n],
            send_sem=list_sem.at[0],
            recv_sem=list_sem.at[1],
            device_id=(node_peer(step), c),
            device_id_type=MESH,
        ).start()

    pre_gate[...] = jnp.zeros_like(pre_gate)
    pre_up[...] = jnp.zeros_like(pre_up)
    raw[...] = jnp.zeros_like(raw)
    score[...] = jnp.zeros_like(score)

    def order(axis):
        i = lax.broadcasted_iota(jnp.int32, (dense, dense), axis)
        by_node = jnp.bitwise_and(i, 7) * 32 + jnp.bitwise_and(jnp.right_shift(i, 3), 1) * 16 + jnp.right_shift(i, 4)
        return jnp.where(by_node == lax.broadcasted_iota(jnp.int32, (dense, dense), 1 - axis), 1.0, 0.0)

    perm[...] = order(0).astype(BF16)
    perm_t[...] = order(1).astype(BF16)

    def wait_bytes(ref, sem):
        pltpu.make_async_copy(ref, ref, sem).wait()

    wait_bytes(lists.at[pl.ds(0, n_node - 1)], list_sem.at[1])

    source = lax.broadcasted_iota(jnp.int32, (8, 1), 0)
    lane_row = lax.broadcasted_iota(jnp.int32, (8, cap), 1)
    lane_slot = lax.broadcasted_iota(jnp.int32, (8, packed), 1)
    used = jnp.zeros((8, 1), jnp.int32)
    expand_parts, row_parts = [], []
    for e in range(n_node):
        listed = jnp.broadcast_to(lists[e], (8, cap))
        mine = jnp.right_shift(listed, 8) == n * n_chip + source
        local_row = jnp.bitwise_and(listed, 255)
        low = jnp.min(jnp.where(mine, local_row, 256), axis=1, keepdims=True)
        high = jnp.max(jnp.where(mine, local_row, -1), axis=1, keepdims=True)
        place = source * BLOCK + used
        first = jnp.where(high >= 0, place, -1)
        second = jnp.where(high > low, place + 8, -1)
        expand_parts.append(jnp.where(lane_slot == first, 1.0, 0.0))
        expand_parts.append(jnp.where(lane_slot == second, 1.0, 0.0))
        row_parts.append(jnp.where(lane_row == low, 1.0, 0.0))
        row_parts.append(jnp.where(lane_row == jnp.where(high > low, high, -1), 1.0, 0.0))
        used = used + jnp.where(high >= 0, 1, 0)
    expand_f32 = jnp.concatenate(expand_parts, axis=0)
    expand[...] = expand_f32.astype(BF16)
    compact[...] = expand_f32.T.astype(BF16)
    row_hot = jnp.concatenate(row_parts, axis=0).astype(BF16)
    full_send[...] = dot(perm_t[...], row_hot).astype(BF16)

    def block(i):
        return pl.ds(pl.multiple_of(i * BLOCK, BLOCK), BLOCK)

    def wide(i):
        return pl.ds(pl.multiple_of(i * 2 * BLOCK, 2 * BLOCK), 2 * BLOCK)

    def turn_to_chips(src, dst, sem, at=slice(None)):
        for step in CHIP_STEPS:
            to = chip_peer(step)
            pltpu.make_async_remote_copy(
                src_ref=src.at[wide(to), at],
                dst_ref=dst.at[wide(c), at],
                send_sem=sem.at[0],
                recv_sem=sem.at[1],
                device_id=(n, to),
                device_id_type=MESH,
            ).start()
        dst[wide(c), at] = src[wide(c), at]

    def turn_done(ref, sem, at=slice(None)):
        wait_bytes(ref.at[pl.ds(0, dense - 2 * BLOCK), at], sem)

    turn_to_chips(full_send, full_mine, full_sem)
    pick_send[...] = dot(compact[...], row_hot).astype(BF16)
    for step in CHIP_STEPS:
        to = chip_peer(step)
        pltpu.make_async_remote_copy(
            src_ref=pick_send.at[block(to), :],
            dst_ref=pick_mine.at[block(c), :],
            send_sem=pick_sem.at[0],
            recv_sem=pick_sem.at[1],
            device_id=(n, to),
            device_id_type=MESH,
        ).start()
    pick_mine[block(c), :] = pick_send[block(c), :]

    def cols(s):
        return pl.ds(pl.multiple_of(s * chunk, chunk), chunk)

    def to_chips(src, dst, s, send_sem, recv_sem):
        for step in CHIP_STEPS:
            to = chip_peer(step)
            pltpu.make_async_remote_copy(
                src_ref=src.at[block(to), cols(s)],
                dst_ref=dst.at[block(c), cols(s)],
                send_sem=send_sem.at[s],
                recv_sem=recv_sem.at[s],
                device_id=(n, to),
                device_id_type=MESH,
            ).start()
        dst[block(c), cols(s)] = src[block(c), cols(s)]

    def to_nodes(src, dst, s, send_sem, recv_sem, src_cols=None, dst_cols=None):
        src_cols = cols(s) if src_cols is None else src_cols
        dst_cols = cols(s) if dst_cols is None else dst_cols
        for step in NODE_STEPS:
            to = node_peer(step)
            pltpu.make_async_remote_copy(
                src_ref=src.at[block(to), src_cols],
                dst_ref=dst.at[block(n), dst_cols],
                send_sem=send_sem.at[s],
                recv_sem=recv_sem.at[s],
                device_id=(to, c),
                device_id_type=MESH,
            ).start()
        dst[block(n), dst_cols] = src[block(n), src_cols]

    def chips_done(ref, s, sem):
        wait_bytes(ref.at[pl.ds(0, packed - BLOCK), cols(s)], sem.at[s])

    def nodes_done(ref, s, sem):
        wait_bytes(ref.at[pl.ds(0, dense - BLOCK), cols(s)], sem.at[s])

    def gather(s):
        stage_a[:, cols(s)] = dot(pick_mine[...], both[:, cols(s)]).astype(BF16)
        to_chips(stage_a, mid, s, a_send, a_recv)

    def forward(s):
        chips_done(mid, s, a_recv)
        stage_b[:, cols(s)] = dot(expand[...], mid[:, cols(s)]).astype(BF16)
        to_nodes(stage_b, rows, s, b_send, b_recv)

    def up_step(s):
        x = rows[:, cols(s)]
        pre_gate[...] += dot(x, w_gate[cols(s), :])
        pre_up[...] += dot(x, w_up[cols(s), :])
        score[...] += dot_nt(x, jnp.broadcast_to(router[:, cols(s)], (128, chunk)))

    def down_step(s):
        nodes_done(rows, s, b_recv)
        raw[...] += dot_nt(rows[:, cols(s)], w_down[:, cols(s - STEPS)])

    def from_x(r, carry):
        part = pl.ds(pl.multiple_of(r * 64, 64), 64)
        s = jax.nn.sigmoid(score[part, :])
        score[part, :] = s
        for j in range(ff // 128):
            lanes = pl.ds(128 * j, 128)
            g = pre_gate[part, lanes]
            u = pre_up[part, lanes]
            sig = jax.nn.sigmoid(g)
            act = g * sig
            hidden[part, lanes] = (act * u).astype(BF16)
            pre_gate[part, lanes] = s * (u * sig * (1.0 + g * (1.0 - sig)))
            pre_up[part, lanes] = s * act
        return carry

    whole = pl.ds(0, chunk)
    turn_done(full_mine, full_sem.at[1])
    full_pick[...] = dot(perm[...], full_mine[...]).astype(BF16)
    loads[0].wait()

    def first_phase(s, carry):
        stage_b[:, cols(s)] = dot(full_pick[...], both[:, cols(s)]).astype(BF16)
        to_nodes(stage_b, first_mid, s, b_send, b_recv)
        return carry

    lax.fori_loop(0, FIRST, first_phase, 0)
    loads[1].wait()
    wait_bytes(pick_mine.at[pl.ds(0, (n_chip - 1) * BLOCK), :], pick_sem.at[1])
    for s in range(FIRST, FIRST + LEAD):
        gather(s)
    scatter[...] = pick_mine[...].astype(F32).T.astype(BF16)
    full_scatter[...] = full_pick[...].astype(F32).T.astype(BF16)

    def phase(t, carry):
        @pl.when(t + LEAD < 2 * STEPS)
        def _():
            gather(t + LEAD)

        @pl.when(t < 2 * STEPS)
        def _():
            forward(t)

        @pl.when(t < 2 * FIRST)
        def _():
            f = t - FIRST
            nodes_done(first_mid, f, b_recv)
            first_turn[:, cols(f)] = dot(perm_t[...], first_mid[:, cols(f)]).astype(BF16)
            turn_to_chips(first_turn, first_got, first_sem.at[f], cols(f))

        @pl.when(t == LAG)
        def _():
            loads[2].wait()
            loads[3].wait()

        @pl.when((t >= LAG) & (t < FIRST + LAG))
        def _():
            f = t - LAG
            turn_done(first_got, first_sem.at[f, 1], cols(f))
            rows[:, cols(f)] = dot(perm[...], first_got[:, cols(f)]).astype(BF16)

        @pl.when((t >= FIRST + LAG) & (t < STEPS + LAG))
        def _():
            nodes_done(rows, t - LAG, b_recv)

        @pl.when((t >= LAG) & (t < STEPS + LAG))
        def _():
            up_step(t - LAG)

        @pl.when(t == STEPS + LAG)
        def _():
            lax.fori_loop(0, dense // 64, from_x, 0)
            loads[4].wait()

        @pl.when(t >= STEPS + LAG)
        def _():
            down_step(t - LAG)

        return carry

    lax.fori_loop(FIRST, 2 * STEPS + LAG, phase, 0)

    def from_dy(r, carry):
        part = pl.ds(pl.multiple_of(r * 64, 64), 64)
        total = jnp.zeros((64, 128), F32)
        for j in range(ff // 128):
            lanes = pl.ds(128 * j, 128)
            v = raw[part, lanes]
            total = total + v * hidden[part, lanes].astype(F32)
            gate_grad[part, lanes] = (v * pre_gate[part, lanes]).astype(BF16)
            up_grad[part, lanes] = (v * pre_up[part, lanes]).astype(BF16)
        s = score[part, :]
        score_grad[part, :] = jnp.sum(total, axis=1, keepdims=True) * s * (1.0 - s)
        return carry

    lax.fori_loop(0, dense // 64, from_dy, 0)

    def pick_chunk(s):
        value = dot_nt(gate_grad[...], w_gate[cols(s), :])
        value = value + dot_nt(up_grad[...], w_up[cols(s), :])
        value = value + score_grad[:, :1] * router[:, cols(s)].astype(F32)
        back[:, cols(s)] = value.astype(BF16)

    def send_back(s):
        pick_chunk(s)
        to_nodes(back, back_mid, s, rb_send, rb_recv)

    def send_home(s):
        nodes_done(back_mid, s, rb_recv)
        back_stage[:, cols(s)] = dot(compact[...], back_mid[:, cols(s)]).astype(BF16)
        to_chips(back_stage, ret, s, ra_send, ra_recv)

    def return_phase(s, carry):
        send_back(s)
        return carry

    final = STEPS - 1
    send_back(0)
    pick_chunk(final)
    last_turn[...] = dot(perm_t[...], back[:, cols(final)]).astype(BF16)
    turn_to_chips(last_turn, last_mid, last_sem)
    lax.fori_loop(1, final, return_phase, 0)
    hidden_t[...] = hidden[...].astype(F32).T.astype(BF16)

    def scale(r, carry):
        part = pl.ds(pl.multiple_of(r * 16, 16), 16)
        s = score[part, :1]
        out_grad[part, :] = (s * rows[part, width:].astype(F32)).astype(BF16)
        return carry

    lax.fori_loop(0, dense // 16, scale, 0)
    def down_phase(r, carry):
        part = pl.ds(pl.multiple_of(r * (ff // 4), 32), ff // 4)
        down_grad[part, :] = dot(hidden_t[part, :], out_grad[...]).astype(BF16)
        return carry

    lax.fori_loop(0, 4, down_phase, 0)

    turn_done(last_mid, last_sem.at[1])
    last_stage[...] = dot(perm[...], last_mid[...]).astype(BF16)
    to_nodes(last_stage, last_got, final, rb_send, rb_recv, whole, whole)

    across = score_grad[...].T[:16, :]
    part0 = across.astype(BF16)
    rest = across - part0.astype(F32)
    part1 = rest.astype(BF16)
    part2 = (rest - part1.astype(F32)).astype(BF16)
    for s in range(STEPS):
        x = rows[:, s * chunk : (s + 1) * chunk]
        value = dot(part0, x) + (dot(part1, x) + dot(part2, x))
        router_grad[:, s * chunk : (s + 1) * chunk] = value[:1, :]

    def home_phase(s, carry):
        send_home(s)
        return carry

    lax.fori_loop(0, final, home_phase, 0)

    def home(s, carry):
        chips_done(ret, s, ra_recv)
        token_grad[:, cols(s)] = dot(scatter[...], ret[:, cols(s)]).astype(BF16)
        return carry

    lax.fori_loop(0, final, home, 0)
    wait_bytes(last_got.at[pl.ds(0, dense - BLOCK), :], rb_recv.at[final])
    token_grad[:, cols(final)] = dot(full_scatter[...], last_got[...]).astype(BF16)
    wait_bytes(lists.at[pl.ds(0, n_node - 1)], list_sem.at[0])
    wait_bytes(pick_mine.at[pl.ds(0, (n_chip - 1) * BLOCK), :], pick_sem.at[0])

    turn_done(full_send, full_sem.at[0])
    for f in range(FIRST):
        turn_done(first_turn, first_sem.at[f, 0], cols(f))
    turn_done(last_turn, last_sem.at[0])
    wait_bytes(last_stage.at[pl.ds(0, dense - BLOCK), :], rb_send.at[final])
    for f in range(FIRST):
        nodes_done(stage_b, f, b_send)

    def drain_out(s, carry):
        chips_done(stage_a, s, a_send)
        nodes_done(stage_b, s, b_send)
        return carry

    def drain_back(s, carry):
        nodes_done(back, s, rb_send)
        chips_done(back_stage, s, ra_send)
        return carry

    lax.fori_loop(FIRST, 2 * STEPS, drain_out, 0)
    lax.fori_loop(0, final, drain_back, 0)


def finish_kernel(token_in, down_in, router_in, token_grad, down_grad, router_grad, sem):
    stores = [
        pltpu.make_async_copy(down_in, down_grad, sem.at[0]),
        pltpu.make_async_copy(token_in, token_grad, sem.at[1]),
        pltpu.make_async_copy(router_in, router_grad, sem.at[2]),
    ]
    for store in stores:
        store.start()
    for store in stores:
        store.wait()


def local(n_node, n_chip, tokens, cotangent, chosen, group, router, w_gate, w_up, w_down):
    row_count, width = tokens.shape
    ff = w_gate.shape[2]
    cap = chosen.shape[1]
    dense = n_node * BLOCK
    packed = n_chip * BLOCK
    vmem = pl.BlockSpec(memory_space=pltpu.VMEM)
    hbm = pl.BlockSpec(memory_space=pl.ANY)
    dma = pltpu.SemaphoreType.DMA
    results = pl.pallas_call(
        functools.partial(exchange_kernel, n_node, n_chip),
        out_shape=[
            pltpu.VMEM((row_count, width), BF16),
            pltpu.VMEM((ff, width), BF16),
            pltpu.VMEM((1, width), F32),
        ],
        in_specs=[hbm, vmem] + [hbm] * 6,
        out_specs=[vmem] * 3,
        scratch_shapes=[
            pltpu.VMEM((1, cap), jnp.int32),
            pltpu.VMEM((1, width), BF16),
            pltpu.VMEM((row_count, 2 * width), BF16),
            pltpu.VMEM((width, ff), BF16),
            pltpu.VMEM((width, ff), BF16),
            pltpu.VMEM((ff, width), BF16),
            pltpu.VMEM((1, cap), jnp.int32),
            pltpu.VMEM((n_node, 1, cap), jnp.int32),
            pltpu.VMEM((dense, packed), BF16),
            pltpu.VMEM((packed, dense), BF16),
            pltpu.VMEM((packed, row_count), BF16),
            pltpu.VMEM((packed, row_count), BF16),
            pltpu.VMEM((packed, 2 * width), BF16),
            pltpu.VMEM((packed, 2 * width), BF16),
            pltpu.VMEM((dense, 2 * width), BF16),
            pltpu.VMEM((dense, 2 * width), BF16),
            pltpu.VMEM((dense, ff), F32),
            pltpu.VMEM((dense, ff), F32),
            pltpu.VMEM((dense, ff), F32),
            pltpu.VMEM((dense, 128), F32),
            pltpu.VMEM((dense, ff), BF16),
            pltpu.VMEM((ff, dense), BF16),
            pltpu.VMEM((dense, ff), BF16),
            pltpu.VMEM((dense, ff), BF16),
            pltpu.VMEM((dense, 128), F32),
            pltpu.VMEM((dense, width), BF16),
            pltpu.VMEM((dense, width), BF16),
            pltpu.VMEM((dense, width), BF16),
            pltpu.VMEM((packed, width), BF16),
            pltpu.VMEM((packed, width), BF16),
            pltpu.VMEM((row_count, packed), BF16),
            pltpu.VMEM((dense, dense), BF16),
            pltpu.VMEM((dense, dense), BF16),
            pltpu.VMEM((dense, row_count), BF16),
            pltpu.VMEM((dense, row_count), BF16),
            pltpu.VMEM((dense, row_count), BF16),
            pltpu.VMEM((row_count, dense), BF16),
            pltpu.VMEM((dense, FIRST * width // STEPS), BF16),
            pltpu.VMEM((dense, FIRST * width // STEPS), BF16),
            pltpu.VMEM((dense, FIRST * width // STEPS), BF16),
            pltpu.VMEM((dense, width // STEPS), BF16),
            pltpu.VMEM((dense, width // STEPS), BF16),
            pltpu.VMEM((dense, width // STEPS), BF16),
            pltpu.VMEM((dense, width // STEPS), BF16),
            dma((7,)),
            dma((2,)),
            dma((2,)),
            dma((2,)),
            dma((FIRST, 2)),
            dma((2,)),
            dma((2 * STEPS,)),
            dma((2 * STEPS,)),
            dma((2 * STEPS,)),
            dma((2 * STEPS,)),
            dma((STEPS,)),
            dma((STEPS,)),
            dma((STEPS,)),
            dma((STEPS,)),
        ],
        compiler_params=pltpu.CompilerParams(
            collective_id=0, has_side_effects=True, vmem_limit_bytes=48 * 1024 * 1024
        ),
        name="exchange",
    )(
        chosen,
        group.reshape(1, 1),
        router,
        tokens,
        cotangent,
        w_gate[0],
        w_up[0],
        w_down[0],
    )
    token_grad, down_grad, router_grad = pl.pallas_call(
        finish_kernel,
        out_shape=[
            jax.ShapeDtypeStruct((row_count, width), BF16),
            jax.ShapeDtypeStruct((ff, width), BF16),
            jax.ShapeDtypeStruct((1, width), F32),
        ],
        in_specs=[vmem] * 3,
        out_specs=[hbm] * 3,
        scratch_shapes=[dma((3,))],
        compiler_params=pltpu.CompilerParams(vmem_limit_bytes=16 * 1024 * 1024),
        name="finish",
    )(*results)
    return token_grad, down_grad[None], router_grad


def solution(mesh):
    rows = P(("node", "chip"), None)
    weight = P(("node", "chip"), None, None)
    return jax.shard_map(
        functools.partial(local, mesh.shape["node"], mesh.shape["chip"]),
        mesh=mesh,
        in_specs=(rows, rows, rows, P(("node", "chip")), rows, weight, weight, weight),
        out_specs=(rows, weight, rows),
        check_vma=False,
    )
```

```python
import functools

import jax
import jax.numpy as jnp
from jax import lax
from jax.experimental import pallas as pl
from jax.experimental.pallas import tpu as pltpu
from jax.sharding import PartitionSpec as P

MESH = pl.DeviceIdType.MESH
F32 = jnp.float32
BF16 = jnp.bfloat16
NODE_STEPS = (
    (2, 2), (3, 2), (2, 3), (1, 2), (2, 1), (0, 2), (2, 0),
    (3, 1), (1, 3), (3, 3), (1, 1), (0, 3), (3, 0), (0, 1), (1, 0),
)
CHIP_STEPS = (5, 4, 3, 2, 7, 6, 1)
BLOCK = 16
STEPS = 4
FIRST = 2
FINAL = 1
LEAD = 2
LAG = 4


def dot(a, b):
    return jnp.dot(a, b, preferred_element_type=F32)


def dot_nt(a, b):
    return lax.dot_general(a, b, (((1,), (1,)), ((), ())), preferred_element_type=F32)


def exchange_kernel(
    n_node,
    n_chip,
    chosen_hbm,
    group,
    router_hbm,
    tokens,
    cotangent,
    w_gate_hbm,
    w_up_hbm,
    w_down_hbm,
    token_grad,
    down_grad,
    router_grad,
    chosen,
    router,
    both,
    w_gate,
    w_up,
    w_down,
    list_send,
    lists,
    expand,
    compact,
    pick_send,
    pick_mine,
    stage_a,
    mid,
    stage_b,
    rows,
    pre_gate,
    pre_up,
    raw,
    score,
    hidden,
    hidden_t,
    gate_grad,
    up_grad,
    score_grad,
    out_grad,
    back,
    back_mid,
    back_stage,
    ret,
    scatter,
    perm,
    perm_t,
    full_send,
    full_mine,
    full_pick,
    full_scatter,
    first_mid,
    first_turn,
    first_got,
    last_turn,
    last_mid,
    last_stage,
    last_got,
    load_sem,
    list_sem,
    pick_sem,
    full_sem,
    first_sem,
    last_sem,
    a_send,
    a_recv,
    b_send,
    b_recv,
    rb_send,
    rb_recv,
    ra_send,
    ra_recv,
):
    n = lax.axis_index("node")
    c = lax.axis_index("chip")
    width = router.shape[1]
    ff = w_gate.shape[1]
    chunk = width // STEPS
    dense = n_node * BLOCK
    packed = n_chip * BLOCK

    small_loads = [
        pltpu.make_async_copy(chosen_hbm, chosen, load_sem.at[5]),
        pltpu.make_async_copy(router_hbm, router, load_sem.at[6]),
    ]
    for load in small_loads:
        load.start()
    loads = [
        pltpu.make_async_copy(tokens, both.at[:, pl.ds(0, width)], load_sem.at[0]),
        pltpu.make_async_copy(cotangent, both.at[:, pl.ds(width, width)], load_sem.at[1]),
        pltpu.make_async_copy(w_gate_hbm, w_gate, load_sem.at[2]),
        pltpu.make_async_copy(w_up_hbm, w_up, load_sem.at[3]),
        pltpu.make_async_copy(w_down_hbm, w_down, load_sem.at[4]),
    ]
    for load in loads:
        load.start()

    def node_peer(step):
        y, z = step
        return lax.rem(n // 4 + y, 4) * 4 + lax.rem(lax.rem(n, 4) + z, 4)

    def chip_peer(i):
        return lax.rem(c + i, n_chip)

    barrier = pltpu.get_barrier_semaphore()

    for step in NODE_STEPS:
        pl.semaphore_signal(barrier, inc=1, device_id=(node_peer(step), c), device_id_type=MESH)
    for step in CHIP_STEPS:
        pl.semaphore_signal(barrier, inc=1, device_id=(n, chip_peer(step)), device_id_type=MESH)

    for load in small_loads:
        load.wait()
    cap = chosen.shape[1]
    slot_index = lax.broadcasted_iota(jnp.int32, (1, cap), 1)
    live = jnp.right_shift(jnp.full((1, cap), cap, jnp.int32), jnp.broadcast_to(group[...], (1, cap)))
    own_list = jnp.where(slot_index < live, chosen[...], -1)
    list_send[...] = own_list
    lists[n] = own_list

    pl.semaphore_wait(barrier, n_node + n_chip - 2)

    for step in NODE_STEPS:
        pltpu.make_async_remote_copy(
            src_ref=list_send,
            dst_ref=lists.at[n],
            send_sem=list_sem.at[0],
            recv_sem=list_sem.at[1],
            device_id=(node_peer(step), c),
            device_id_type=MESH,
        ).start()

    pre_gate[...] = jnp.zeros_like(pre_gate)
    pre_up[...] = jnp.zeros_like(pre_up)
    raw[...] = jnp.zeros_like(raw)
    score[...] = jnp.zeros_like(score)

    def order(axis):
        i = lax.broadcasted_iota(jnp.int32, (dense, dense), axis)
        by_node = jnp.bitwise_and(i, 7) * 32 + jnp.bitwise_and(jnp.right_shift(i, 3), 1) * 16 + jnp.right_shift(i, 4)
        return jnp.where(by_node == lax.broadcasted_iota(jnp.int32, (dense, dense), 1 - axis), 1.0, 0.0)

    perm[...] = order(0).astype(BF16)
    perm_t[...] = order(1).astype(BF16)

    def wait_bytes(ref, sem):
        pltpu.make_async_copy(ref, ref, sem).wait()

    wait_bytes(lists.at[pl.ds(0, n_node - 1)], list_sem.at[1])

    source = lax.broadcasted_iota(jnp.int32, (8, 1), 0)
    lane_row = lax.broadcasted_iota(jnp.int32, (8, cap), 1)
    lane_slot = lax.broadcasted_iota(jnp.int32, (8, packed), 1)
    used = jnp.zeros((8, 1), jnp.int32)
    expand_parts, row_parts, number_parts = [], [], []
    for e in range(n_node):
        listed = jnp.broadcast_to(lists[e], (8, cap))
        mine = jnp.right_shift(listed, 8) == n * n_chip + source
        local_row = jnp.bitwise_and(listed, 255)
        low = jnp.min(jnp.where(mine, local_row, 256), axis=1, keepdims=True)
        high = jnp.max(jnp.where(mine, local_row, -1), axis=1, keepdims=True)
        place = source * BLOCK + used
        first = jnp.where(high >= 0, place, -1)
        second = jnp.where(high > low, place + 8, -1)
        expand_parts.append(jnp.where(lane_slot == first, 1.0, 0.0))
        expand_parts.append(jnp.where(lane_slot == second, 1.0, 0.0))
        row_parts.append(jnp.where(lane_row == low, 1.0, 0.0))
        row_parts.append(jnp.where(lane_row == high, 1.0, 0.0))
        number_parts.append(jnp.broadcast_to(jnp.where(high >= 0, low, -1), (8, 128)))
        number_parts.append(jnp.broadcast_to(jnp.where(high > low, high, -1), (8, 128)))
        used = used + jnp.where(high >= 0, 1, 0)
    numbers = jnp.concatenate(number_parts, axis=0).astype(F32).astype(BF16)
    full_send[...] = dot(perm_t[...], numbers).astype(BF16)

    def block(i):
        return pl.ds(pl.multiple_of(i * BLOCK, BLOCK), BLOCK)

    def wide(i):
        return pl.ds(pl.multiple_of(i * 2 * BLOCK, 2 * BLOCK), 2 * BLOCK)

    def turn_to_chips(src, dst, sem, at=slice(None)):
        for step in CHIP_STEPS:
            to = chip_peer(step)
            pltpu.make_async_remote_copy(
                src_ref=src.at[wide(to), at],
                dst_ref=dst.at[wide(c), at],
                send_sem=sem.at[0],
                recv_sem=sem.at[1],
                device_id=(n, to),
                device_id_type=MESH,
            ).start()
        dst[wide(c), at] = src[wide(c), at]

    def turn_done(ref, sem, at=slice(None)):
        wait_bytes(ref.at[pl.ds(0, dense - 2 * BLOCK), at], sem)

    turn_to_chips(full_send, full_mine, full_sem)
    expand_f32 = jnp.concatenate(expand_parts, axis=0)
    expand[...] = expand_f32.astype(BF16)
    compact[...] = expand_f32.T.astype(BF16)
    row_hot = jnp.concatenate(row_parts, axis=0).astype(BF16)
    pick_send[...] = dot(compact[...], row_hot).astype(BF16)
    for step in CHIP_STEPS:
        to = chip_peer(step)
        pltpu.make_async_remote_copy(
            src_ref=pick_send.at[block(to), :],
            dst_ref=pick_mine.at[block(c), :],
            send_sem=pick_sem.at[0],
            recv_sem=pick_sem.at[1],
            device_id=(n, to),
            device_id_type=MESH,
        ).start()
    pick_mine[block(c), :] = pick_send[block(c), :]

    def cols(s):
        return pl.ds(pl.multiple_of(s * chunk, chunk), chunk)

    def to_chips(src, dst, s, send_sem, recv_sem):
        for step in CHIP_STEPS:
            to = chip_peer(step)
            pltpu.make_async_remote_copy(
                src_ref=src.at[block(to), cols(s)],
                dst_ref=dst.at[block(c), cols(s)],
                send_sem=send_sem.at[s],
                recv_sem=recv_sem.at[s],
                device_id=(n, to),
                device_id_type=MESH,
            ).start()
        dst[block(c), cols(s)] = src[block(c), cols(s)]

    def to_nodes(src, dst, s, send_sem, recv_sem, src_cols=None, dst_cols=None):
        src_cols = cols(s) if src_cols is None else src_cols
        dst_cols = cols(s) if dst_cols is None else dst_cols
        for step in NODE_STEPS:
            to = node_peer(step)
            pltpu.make_async_remote_copy(
                src_ref=src.at[block(to), src_cols],
                dst_ref=dst.at[block(n), dst_cols],
                send_sem=send_sem.at[s],
                recv_sem=recv_sem.at[s],
                device_id=(to, c),
                device_id_type=MESH,
            ).start()
        dst[block(n), dst_cols] = src[block(n), src_cols]

    def chips_done(ref, s, sem):
        wait_bytes(ref.at[pl.ds(0, packed - BLOCK), cols(s)], sem.at[s])

    def nodes_done(ref, s, sem):
        wait_bytes(ref.at[pl.ds(0, dense - BLOCK), cols(s)], sem.at[s])

    def gather(s):
        stage_a[:, cols(s)] = dot(pick_mine[...], both[:, cols(s)]).astype(BF16)
        to_chips(stage_a, mid, s, a_send, a_recv)

    def forward(s):
        chips_done(mid, s, a_recv)
        stage_b[:, cols(s)] = dot(expand[...], mid[:, cols(s)]).astype(BF16)
        to_nodes(stage_b, rows, s, b_send, b_recv)

    def up_step(s):
        x = rows[:, cols(s)]
        pre_gate[...] += dot(x, w_gate[cols(s), :])
        pre_up[...] += dot(x, w_up[cols(s), :])
        score[...] += dot_nt(x, jnp.broadcast_to(router[:, cols(s)], (128, chunk)))

    def down_step(s):
        nodes_done(rows, s, b_recv)
        raw[...] += dot_nt(rows[:, cols(s)], w_down[:, cols(s - STEPS)])

    def from_x(r, carry):
        part = pl.ds(pl.multiple_of(r * 64, 64), 64)
        s = jax.nn.sigmoid(score[part, :])
        score[part, :] = s
        for j in range(ff // 128):
            lanes = pl.ds(128 * j, 128)
            g = pre_gate[part, lanes]
            u = pre_up[part, lanes]
            sig = jax.nn.sigmoid(g)
            act = g * sig
            hidden[part, lanes] = (act * u).astype(BF16)
            pre_gate[part, lanes] = s * (u * sig * (1.0 + g * (1.0 - sig)))
            pre_up[part, lanes] = s * act
        return carry

    turn_done(full_mine, full_sem.at[1])
    wanted = dot(perm[...], full_mine[...])
    lane = lax.broadcasted_iota(jnp.int32, (dense, 128), 1).astype(F32)
    for h in range(full_pick.shape[1] // 128):
        full_pick[:, 128 * h : 128 * (h + 1)] = jnp.where(wanted == lane + 128.0 * h, 1.0, 0.0).astype(BF16)
    loads[0].wait()

    def first_phase(s, carry):
        stage_b[:, cols(s)] = dot(full_pick[...], both[:, cols(s)]).astype(BF16)
        to_nodes(stage_b, first_mid, s, b_send, b_recv)
        return carry

    lax.fori_loop(0, FIRST, first_phase, 0)
    loads[1].wait()
    wait_bytes(pick_mine.at[pl.ds(0, (n_chip - 1) * BLOCK), :], pick_sem.at[1])
    for s in range(FIRST, FIRST + LEAD):
        gather(s)
    scatter[...] = pick_mine[...].astype(F32).T.astype(BF16)
    full_scatter[...] = full_pick[...].astype(F32).T.astype(BF16)

    def phase(t, carry):
        @pl.when(t + LEAD < 2 * STEPS)
        def _():
            gather(t + LEAD)

        @pl.when(t < 2 * STEPS)
        def _():
            forward(t)

        @pl.when(t < 2 * FIRST)
        def _():
            f = t - FIRST
            nodes_done(first_mid, f, b_recv)
            first_turn[:, cols(f)] = dot(perm_t[...], first_mid[:, cols(f)]).astype(BF16)
            turn_to_chips(first_turn, first_got, first_sem.at[f], cols(f))

        @pl.when(t == LAG)
        def _():
            loads[2].wait()
            loads[3].wait()

        @pl.when((t >= LAG) & (t < FIRST + LAG))
        def _():
            f = t - LAG
            turn_done(first_got, first_sem.at[f, 1], cols(f))
            rows[:, cols(f)] = dot(perm[...], first_got[:, cols(f)]).astype(BF16)

        @pl.when((t >= FIRST + LAG) & (t < STEPS + LAG))
        def _():
            nodes_done(rows, t - LAG, b_recv)

        @pl.when((t >= LAG) & (t < STEPS + LAG))
        def _():
            up_step(t - LAG)

        @pl.when(t == STEPS + LAG)
        def _():
            lax.fori_loop(0, dense // 64, from_x, 0)
            loads[4].wait()

        @pl.when(t >= STEPS + LAG)
        def _():
            down_step(t - LAG)

        return carry

    lax.fori_loop(FIRST, 2 * STEPS + LAG, phase, 0)

    def from_dy(r, carry):
        part = pl.ds(pl.multiple_of(r * 64, 64), 64)
        total = jnp.zeros((64, 128), F32)
        for j in range(ff // 128):
            lanes = pl.ds(128 * j, 128)
            v = raw[part, lanes]
            total = total + v * hidden[part, lanes].astype(F32)
            gate_grad[part, lanes] = (v * pre_gate[part, lanes]).astype(BF16)
            up_grad[part, lanes] = (v * pre_up[part, lanes]).astype(BF16)
        s = score[part, :]
        score_grad[part, :] = jnp.sum(total, axis=1, keepdims=True) * s * (1.0 - s)
        return carry

    lax.fori_loop(0, dense // 64, from_dy, 0)

    def pick_chunk(s):
        value = dot_nt(gate_grad[...], w_gate[cols(s), :])
        value = value + dot_nt(up_grad[...], w_up[cols(s), :])
        value = value + score_grad[:, :1] * router[:, cols(s)].astype(F32)
        back[:, cols(s)] = value.astype(BF16)

    def send_back(s):
        pick_chunk(s)
        to_nodes(back, back_mid, s, rb_send, rb_recv)

    def send_home(s):
        nodes_done(back_mid, s, rb_recv)
        back_stage[:, cols(s)] = dot(compact[...], back_mid[:, cols(s)]).astype(BF16)
        to_chips(back_stage, ret, s, ra_send, ra_recv)

    def return_phase(s, carry):
        send_back(s)
        return carry

    final = STEPS - FINAL

    def final_turn(f, carry):
        pick_chunk(final + f)
        last_turn[:, cols(f)] = dot(perm_t[...], back[:, cols(final + f)]).astype(BF16)
        turn_to_chips(last_turn, last_mid, last_sem.at[f], cols(f))
        return carry

    def final_phase(f, carry):
        turn_done(last_mid, last_sem.at[f, 1], cols(f))
        last_stage[:, cols(f)] = dot(perm[...], last_mid[:, cols(f)]).astype(BF16)
        to_nodes(last_stage, last_got, final + f, rb_send, rb_recv, cols(f), cols(f))
        return carry

    lax.fori_loop(0, FINAL, return_phase, 0)
    lax.fori_loop(0, FINAL, final_turn, 0)
    lax.fori_loop(FINAL, final, return_phase, 0)
    hidden_t[...] = hidden[...].astype(F32).T.astype(BF16)

    def scale(r, carry):
        part = pl.ds(pl.multiple_of(r * 16, 16), 16)
        s = score[part, :1]
        out_grad[part, :] = (s * rows[part, width:].astype(F32)).astype(BF16)
        return carry

    lax.fori_loop(0, dense // 16, scale, 0)
    def down_phase(r, carry):
        part = pl.ds(pl.multiple_of(r * (ff // 4), 32), ff // 4)
        down_grad[part, :] = dot(hidden_t[part, :], out_grad[...]).astype(BF16)
        return carry

    lax.fori_loop(0, 4, down_phase, 0)

    lax.fori_loop(0, FINAL, final_phase, 0)

    across = score_grad[...].T[:16, :]
    part0 = across.astype(BF16)
    rest = across - part0.astype(F32)
    part1 = rest.astype(BF16)
    part2 = (rest - part1.astype(F32)).astype(BF16)
    for s in range(STEPS):
        x = rows[:, s * chunk : (s + 1) * chunk]
        value = dot(part0, x) + (dot(part1, x) + dot(part2, x))
        router_grad[:, s * chunk : (s + 1) * chunk] = value[:1, :]

    def home_phase(s, carry):
        send_home(s)
        return carry

    lax.fori_loop(0, final, home_phase, 0)

    def home(s, carry):
        chips_done(ret, s, ra_recv)
        token_grad[:, cols(s)] = dot(scatter[...], ret[:, cols(s)]).astype(BF16)
        return carry

    lax.fori_loop(0, final, home, 0)

    def final_home(f, carry):
        wait_bytes(last_got.at[pl.ds(0, dense - BLOCK), cols(f)], rb_recv.at[final + f])
        token_grad[:, cols(final + f)] = dot(full_scatter[...], last_got[:, cols(f)]).astype(BF16)
        return carry

    lax.fori_loop(0, FINAL, final_home, 0)
    wait_bytes(lists.at[pl.ds(0, n_node - 1)], list_sem.at[0])
    wait_bytes(pick_mine.at[pl.ds(0, (n_chip - 1) * BLOCK), :], pick_sem.at[0])

    turn_done(full_send, full_sem.at[0])
    for f in range(FIRST):
        turn_done(first_turn, first_sem.at[f, 0], cols(f))
    for f in range(FINAL):
        turn_done(last_turn, last_sem.at[f, 0], cols(f))
        wait_bytes(last_stage.at[pl.ds(0, dense - BLOCK), cols(f)], rb_send.at[final + f])
    for f in range(FIRST):
        nodes_done(stage_b, f, b_send)

    def drain_out(s, carry):
        chips_done(stage_a, s, a_send)
        nodes_done(stage_b, s, b_send)
        return carry

    def drain_back(s, carry):
        nodes_done(back, s, rb_send)
        chips_done(back_stage, s, ra_send)
        return carry

    lax.fori_loop(FIRST, 2 * STEPS, drain_out, 0)
    lax.fori_loop(0, final, drain_back, 0)


def finish_kernel(token_in, down_in, router_in, token_grad, down_grad, router_grad, sem):
    stores = [
        pltpu.make_async_copy(down_in, down_grad, sem.at[0]),
        pltpu.make_async_copy(token_in, token_grad, sem.at[1]),
        pltpu.make_async_copy(router_in, router_grad, sem.at[2]),
    ]
    for store in stores:
        store.start()
    for store in stores:
        store.wait()


def local(n_node, n_chip, tokens, cotangent, chosen, group, router, w_gate, w_up, w_down):
    row_count, width = tokens.shape
    ff = w_gate.shape[2]
    cap = chosen.shape[1]
    dense = n_node * BLOCK
    packed = n_chip * BLOCK
    vmem = pl.BlockSpec(memory_space=pltpu.VMEM)
    hbm = pl.BlockSpec(memory_space=pl.ANY)
    dma = pltpu.SemaphoreType.DMA
    results = pl.pallas_call(
        functools.partial(exchange_kernel, n_node, n_chip),
        out_shape=[
            pltpu.VMEM((row_count, width), BF16),
            pltpu.VMEM((ff, width), BF16),
            pltpu.VMEM((1, width), F32),
        ],
        in_specs=[hbm, vmem] + [hbm] * 6,
        out_specs=[vmem] * 3,
        scratch_shapes=[
            pltpu.VMEM((1, cap), jnp.int32),
            pltpu.VMEM((1, width), BF16),
            pltpu.VMEM((row_count, 2 * width), BF16),
            pltpu.VMEM((width, ff), BF16),
            pltpu.VMEM((width, ff), BF16),
            pltpu.VMEM((ff, width), BF16),
            pltpu.VMEM((1, cap), jnp.int32),
            pltpu.VMEM((n_node, 1, cap), jnp.int32),
            pltpu.VMEM((dense, packed), BF16),
            pltpu.VMEM((packed, dense), BF16),
            pltpu.VMEM((packed, row_count), BF16),
            pltpu.VMEM((packed, row_count), BF16),
            pltpu.VMEM((packed, 2 * width), BF16),
            pltpu.VMEM((packed, 2 * width), BF16),
            pltpu.VMEM((dense, 2 * width), BF16),
            pltpu.VMEM((dense, 2 * width), BF16),
            pltpu.VMEM((dense, ff), F32),
            pltpu.VMEM((dense, ff), F32),
            pltpu.VMEM((dense, ff), F32),
            pltpu.VMEM((dense, 128), F32),
            pltpu.VMEM((dense, ff), BF16),
            pltpu.VMEM((ff, dense), BF16),
            pltpu.VMEM((dense, ff), BF16),
            pltpu.VMEM((dense, ff), BF16),
            pltpu.VMEM((dense, 128), F32),
            pltpu.VMEM((dense, width), BF16),
            pltpu.VMEM((dense, width), BF16),
            pltpu.VMEM((dense, width), BF16),
            pltpu.VMEM((packed, width), BF16),
            pltpu.VMEM((packed, width), BF16),
            pltpu.VMEM((row_count, packed), BF16),
            pltpu.VMEM((dense, dense), BF16),
            pltpu.VMEM((dense, dense), BF16),
            pltpu.VMEM((dense, 128), BF16),
            pltpu.VMEM((dense, 128), BF16),
            pltpu.VMEM((dense, row_count), BF16),
            pltpu.VMEM((row_count, dense), BF16),
            pltpu.VMEM((dense, FIRST * width // STEPS), BF16),
            pltpu.VMEM((dense, FIRST * width // STEPS), BF16),
            pltpu.VMEM((dense, FIRST * width // STEPS), BF16),
            pltpu.VMEM((dense, FINAL * width // STEPS), BF16),
            pltpu.VMEM((dense, FINAL * width // STEPS), BF16),
            pltpu.VMEM((dense, FINAL * width // STEPS), BF16),
            pltpu.VMEM((dense, FINAL * width // STEPS), BF16),
            dma((7,)),
            dma((2,)),
            dma((2,)),
            dma((2,)),
            dma((FIRST, 2)),
            dma((FINAL, 2)),
            dma((2 * STEPS,)),
            dma((2 * STEPS,)),
            dma((2 * STEPS,)),
            dma((2 * STEPS,)),
            dma((STEPS,)),
            dma((STEPS,)),
            dma((STEPS,)),
            dma((STEPS,)),
        ],
        compiler_params=pltpu.CompilerParams(
            collective_id=0, has_side_effects=True, vmem_limit_bytes=48 * 1024 * 1024
        ),
        name="exchange",
    )(
        chosen,
        group.reshape(1, 1),
        router,
        tokens,
        cotangent,
        w_gate[0],
        w_up[0],
        w_down[0],
    )
    token_grad, down_grad, router_grad = pl.pallas_call(
        finish_kernel,
        out_shape=[
            jax.ShapeDtypeStruct((row_count, width), BF16),
            jax.ShapeDtypeStruct((ff, width), BF16),
            jax.ShapeDtypeStruct((1, width), F32),
        ],
        in_specs=[vmem] * 3,
        out_specs=[hbm] * 3,
        scratch_shapes=[dma((3,))],
        compiler_params=pltpu.CompilerParams(vmem_limit_bytes=16 * 1024 * 1024),
        name="finish",
    )(*results)
    return token_grad, down_grad[None], router_grad


def solution(mesh):
    rows = P(("node", "chip"), None)
    weight = P(("node", "chip"), None, None)
    return jax.shard_map(
        functools.partial(local, mesh.shape["node"], mesh.shape["chip"]),
        mesh=mesh,
        in_specs=(rows, rows, rows, P(("node", "chip")), rows, weight, weight, weight),
        out_specs=(rows, weight, rows),
        check_vma=False,
    )
```
